32 devices in a mesh: groups: 2 (over y), units: 8 (over z, core), cuts: 2 (over x).
Axes of the slice: x: 2, y: 2, z: 4, core: 2. Of those that a mesh axis runs over, the one named last changes fastest.
Arguments:
- residual: bfloat16 [256, 6144], P('groups', 'units'), parts along dimension 0, may hold values from -6 to 6
- query: bfloat16 [256, 6144], P(('groups', 'units'), 'cuts'), parts along dimension 0, may hold values from -48 to 48
- key_cache: bfloat16 [256, 512, 1024], P(('groups', 'units'), None, 'cuts'), parts along dimension 0, may hold values from -8 to 8
- value_cache: bfloat16 [256, 512, 1024], P(('groups', 'units'), None, 'cuts'), parts along dimension 0, may hold values from -7 to 7
- new_key: bfloat16 [256, 1024], P(('groups', 'units'), 'cuts'), parts along dimension 0, may hold values from -8 to 8
- new_value: bfloat16 [256, 1024], P(('groups', 'units'), 'cuts'), parts along dimension 0, may hold values from -6 to 6
- lengths: int32 [256], P(('groups', 'units')), parts along dimension 0, may hold values from 1 to 512, 32768 in all
- out_weight: bfloat16 [6144, 6144], P('cuts', 'units'), may hold values from -1 to 1
- router_weight: float32 [6144, 4], P('units'), may hold values from -0.078125 to 0.078125
- norm_gain: float32 [6144], P('units'), may hold values from 0.5 to 1.5
- expert_ids: int32 [256, 2], P('groups'), parts along dimension 0, may hold values from 0 to 3, all different within a row; in each aligned block of 128 rows (0 to 127, 128 to 255, ...) at most 80 rows name the same one
- gate_weight: bfloat16 [6144, 32768], P(None, ('units', 'cuts')), may hold values from -0.078125 to 0.078125
- up_weight: bfloat16 [6144, 32768], P(None, ('units', 'cuts')), may hold values from -0.078125 to 0.078125
- down_weight: bfloat16 [32768, 6144], P(('units', 'cuts')), may hold values from -0.1875 to 0.1875
Outputs:
- mixed: bfloat16 [256, 6144], P('groups', 'units'), parts along dimension 0
The draws below stay inside these ranges and needn't reach their ends.
There are 2 independent parts, one for each index of `groups`. The reference program is written for one: setup_inputs(seed, part) draws one part's arguments, and reference() takes and returns one part's arrays. A program takes and returns all parts, laid end to end along the dimension named above; an argument that names none is the same for every part. Nothing has to cross between parts.
Inputs may be any that keep to these rules, and one draw needn't show every extreme that they name: `expert_ids`: each row names two different experts; no expert is named by more than 80 rows, and one is named by exactly 80.
All inputs are finite; a program needn't handle non-finite values. No bound on the sum of `lengths` on one device may be relied on, other than what follows from the above.
Results may differ from the reference program's by a relative error of at most 0.013.
Values may be sent and summed in bfloat16 or wider, within the bound.
A program may use at most 192 MiB of HBM per device.

```python
import math
import jax
import jax.numpy as jnp
import numpy as np
from jax import lax

D = 6144
HEADS = 48
KV_HEADS = 8
HD = 128
EXPERTS = 4
FF = 8192
TOP = 2
CACHE_LEN = 512
ROWS = 128
CAP = 80


def feature_signs(count):
    index = jnp.arange(count, dtype=jnp.int32)
    return jnp.where(index * 40503 % 65536 >= 32768, 1.0, -1.0).astype(jnp.float32)


def draw_key_cache(key, part):
    key = jax.random.fold_in(key, 11)
    stored = jnp.clip(jax.random.normal(key, (ROWS, CACHE_LEN, KV_HEADS * HD), jnp.float32), -6.0, 6.0)
    return stored.astype(jnp.bfloat16)


def draw_new_key(key, part):
    key = jax.random.fold_in(key, 12)
    jitter = jnp.clip(jax.random.normal(key, (ROWS, KV_HEADS * HD), jnp.float32), -6.0, 6.0)
    result = jitter
    return result.astype(jnp.bfloat16)


def draw_query(key, part):
    key = jax.random.fold_in(key, 13)
    result = jnp.clip(jax.random.normal(key, (ROWS, HEADS * HD), jnp.float32), -6.0, 6.0)
    return result.astype(jnp.bfloat16)


def draw_residual(key, part):
    key = jax.random.fold_in(key, 14)
    column_scale = 1.0 + 2.0 * jnp.arange(D, dtype=jnp.float32) / (D - 1)
    values = jnp.clip(jax.random.normal(key, (ROWS, D), jnp.float32), -6.0, 6.0)
    result = 0.25 * values * column_scale[None, :]
    return result.astype(jnp.bfloat16)


def draw_value_cache(key, part):
    key = jax.random.fold_in(key, 15)
    noise = jnp.clip(jax.random.normal(key, (ROWS, CACHE_LEN, KV_HEADS * HD), jnp.float32), -6.0, 6.0)
    magnitude = jnp.exp(jax.random.uniform(jax.random.fold_in(key, 1), (ROWS,), jnp.float32, jnp.log(0.2), jnp.log(0.8)))
    direction_sign = jnp.where(jax.random.bernoulli(jax.random.fold_in(key, 2), 0.5, (ROWS,)), 1.0, -1.0)
    offset = (magnitude * direction_sign)[:, None, None] * feature_signs(KV_HEADS * HD)[None, None, :]
    return (noise + offset).astype(jnp.bfloat16)


def draw_out_weight(key, part):
    key = jax.random.fold_in(key, 16)
    fan = HEADS * HD
    noise = jnp.clip(jax.random.normal(key, (fan, D), jnp.float32), -6.0, 6.0) * fan ** (-0.5)
    column_dir = jnp.clip(jax.random.normal(jax.random.fold_in(key, 1), (D,), jnp.float32), -4.0, 4.0)
    share = HEADS // KV_HEADS
    signs = feature_signs(KV_HEADS * HD).reshape(KV_HEADS, 1, HD)
    pattern = jnp.broadcast_to(signs, (KV_HEADS, share, HD)).reshape(fan)
    return (noise + 1.5 / fan * pattern[:, None] * column_dir[None, :]).astype(jnp.bfloat16)


def spiked(values, rng, source, target, parts, factor):
    owner, partner = [(jnp.arange(values.shape[position]) // (values.shape[position] // parts)).reshape([-1 if axis == position else 1 for axis in range(values.ndim)]) for position in (source, target)]
    chosen = jax.random.permutation(rng, parts)[partner]
    strong = (owner == chosen) | (owner == (partner + parts // 2) % parts)
    return jnp.where(strong, factor * values, values)


def level_of(key, dims, cuts, low, top_value):
    level, own = 1.0, jax.random.fold_in(key, 6)
    for dim, parts in cuts:
        draws = jnp.exp(jax.random.uniform(jax.random.fold_in(own, dim), (parts,), jnp.float32, low / len(cuts), top_value / len(cuts)))
        level = level * jnp.repeat(draws, dims[dim] // parts).reshape([-1 if axis == dim else 1 for axis in range(len(dims))])
    return level


def length_profile(number_of, total, limit, skew):
    loads = [(1 << 20) // math.isqrt(grade ** skew) + 1 for grade in range(2, number_of + 1)]
    spare, holding = total - limit - (number_of - 1), [1] * (number_of - 1)
    while spare > 0:
        free = [i for i in range(number_of - 1) if holding[i] < limit]
        pool, budget = sum([loads[i] for i in free]), spare
        for i in free:
            more = min(limit - holding[i], max(1, budget * loads[i] // pool), spare)
            holding[i] = holding[i] + more
            spare = spare - more
    return np.array([limit] + holding)


def ragged_sizes(key, amount, total, reach, slope):
    if amount == 2:
        one = jax.random.randint(key, (), max(1, total - reach), min(reach, total - 1) + 1)
        return jnp.stack([one, total - one])
    sizes = jnp.asarray(length_profile(amount, total, reach, slope), jnp.int32)
    couples = (amount - 1) // 2
    source_of, taker = sizes[1:1 + 2 * couples:2], sizes[2:2 + 2 * couples:2]
    slack = jnp.minimum(source_of - 1, reach - taker)
    shifted = jax.random.randint(jax.random.fold_in(key, 1), (couples,), 0, 1 << 20) % (slack + 1)
    sizes = sizes.at[1:1 + 2 * couples:2].set(source_of - shifted).at[2:2 + 2 * couples:2].set(taker + shifted)
    return sizes[jax.random.permutation(jax.random.fold_in(key, 2), amount)]


def routed_block(own_key, own, number, rows, number_of, top, most, slope):
    order = jax.random.permutation(own_key, number_of)
    heavy_load, usual = shares(number_of, rows * top, most, slope, True), shares(number_of, rows * top, most, slope, False)
    places = jnp.arange(number_of)

    def named(sizes, offset_by):
        used = int((sizes > 0).sum())
        fixed = max(1, used // 4)
        moved = fixed + (places - fixed + offset_by * (used - fixed)) % max(1, number_of - fixed)
        return jnp.zeros((number_of,), jnp.int32).at[order[jnp.where(places < fixed, places, moved)]].set(jnp.asarray(sizes, jnp.int32))

    sizes = jnp.where(number % 4 == 0, named(heavy_load, number // 4), named(usual, number - number // 4 - 1))
    mixed = jax.random.permutation(jax.random.fold_in(own, 3), number_of)
    giver, receiver = mixed[0:number_of // 2 * 2:2], mixed[1:number_of // 2 * 2:2]
    slack = jnp.minimum(sizes[giver] - 1, most - sizes[receiver]) // 2
    slack = jnp.where((giver == order[0]) | (receiver == order[0]) | (sizes[receiver] == 0), 0, jnp.maximum(slack, 0))
    moved = jax.random.randint(jax.random.fold_in(own, 4), (number_of // 2,), 0, 1 << 20) % (slack + 1)
    sizes = sizes.at[giver].add(-moved).at[receiver].add(moved)
    members = jnp.searchsorted(jnp.cumsum(sizes), jnp.arange(rows * top), side="right").astype(jnp.int32)
    table = members.reshape(top, rows).T
    table = table[jax.random.permutation(jax.random.fold_in(own, 1), rows)]
    offset_by = jax.random.randint(jax.random.fold_in(own, 2), (rows, 1), 0, top)
    return jnp.take_along_axis(table, (jnp.arange(top)[None, :] + offset_by) % top, axis=1)


def shares(number_of, total, bound, lean, full):
    weights = [(1 << 20) // math.isqrt(rank ** lean) + 1 for rank in range(1, number_of + 1)]
    largest = bound if full else min(bound, max(-(-total // number_of), total * weights[0] // sum(weights)))
    least = 1 if total - largest >= number_of - 1 else 0
    given, spare = [largest] + [least] * (number_of - 1), total - largest - least * (number_of - 1)
    while spare > 0:
        free = [i for i in range(1, number_of) if given[i] < largest] or [i for i in range(1, number_of) if given[i] < bound]
        whole, left = sum([weights[i] for i in free]), spare
        for i in free:
            more = min(bound - given[i], max(1, left * weights[i] // whole), spare)
            given[i] = given[i] + more
            spare = spare - more
    return np.array(given)


def gaussian(own_key, extent, deviation, limit, shards=(), held_as=jnp.bfloat16):
    loudness = level_of(own_key, extent, shards, -0.22, 0.18) if shards else 1.0
    drawn = jax.random.normal(own_key, extent, jnp.float32) * deviation * loudness
    return jnp.minimum(jnp.maximum(drawn, -limit), limit).astype(held_as)


def gaussian_with(own_key, extent, spread, limit, cuts, heavy, held_as=jnp.bfloat16):
    values = spread * jax.random.normal(own_key, extent, jnp.float32)
    if cuts:
        values = values * level_of(own_key, extent, cuts, -0.22, 0.18)
    return jnp.clip(spiked(values, jax.random.fold_in(own_key, 3), *heavy), -limit, limit).astype(held_as)


def setup_inputs(seed: int = 0, part: int = 0) -> dict:
    seeds = jax.random.split(jax.random.key(seed), 15)
    own_keys = jax.random.split(jax.random.fold_in(seeds[14], part), 15)
    residual = draw_residual(jax.random.fold_in(jax.random.fold_in(seeds[14], part), 71), part)
    query = draw_query(jax.random.fold_in(jax.random.fold_in(seeds[14], part), 71), part)
    key_cache = draw_key_cache(jax.random.fold_in(jax.random.fold_in(seeds[14], part), 71), part)
    value_cache = draw_value_cache(jax.random.fold_in(jax.random.fold_in(seeds[14], part), 71), part)
    new_key = draw_new_key(jax.random.fold_in(jax.random.fold_in(seeds[14], part), 71), part)
    new_value = gaussian(own_keys[5], (ROWS, KV_HEADS * HD), 1.0, 6.0, ((0, 8), (1, 2)))
    lengths = ragged_sizes(own_keys[6], ROWS, ROWS * CACHE_LEN // 2, CACHE_LEN, 2).astype(jnp.int32)
    out_weight = draw_out_weight(jax.random.fold_in(seeds[14], 71), part)
    router_weight = gaussian(seeds[8], (D, EXPERTS), D ** -0.5, 0.078125, ((0, 8),), jnp.float32)
    norm_gain = jnp.clip(1.0 + 0.1 * jax.random.normal(seeds[9], (D,), jnp.float32), 0.5, 1.5)
    expert_ids_keys = jax.random.split(jax.random.fold_in(own_keys[10], 1), ROWS // ROWS)
    expert_ids_turns = jax.random.permutation(jax.random.fold_in(own_keys[10], 3), ROWS // ROWS)
    expert_ids = jax.vmap(lambda own, number: routed_block(jax.random.fold_in(own_keys[10], 2), own, number, ROWS, EXPERTS, TOP, CAP, 2))(expert_ids_keys, expert_ids_turns).reshape((ROWS, TOP))
    gate_weight = gaussian(seeds[11], (D, EXPERTS * FF), D ** -0.5, 0.078125, ((1, 16),))
    up_weight = gaussian(seeds[12], (D, EXPERTS * FF), D ** -0.5, 0.078125, ((1, 16),))
    down_weight = gaussian_with(seeds[13], (EXPERTS * FF, D), (FF // 4) ** -0.5, 0.1875, ((0, 16),), (0, 1, 16, 2.0))
    return {"residual": residual, "query": query, "key_cache": key_cache, "value_cache": value_cache, "new_key": new_key, "new_value": new_value, "lengths": lengths, "out_weight": out_weight, "router_weight": router_weight, "norm_gain": norm_gain, "expert_ids": expert_ids, "gate_weight": gate_weight, "up_weight": up_weight, "down_weight": down_weight}


eps = 1e-05

def reference(residual, query, key_cache, value_cache, new_key, new_value, lengths, out_weight, router_weight, norm_gain, expert_ids, gate_weight, up_weight, down_weight):
    share = HEADS // KV_HEADS
    scale_factor = HD ** (-0.5)
    q_heads = query.astype(jnp.float32).reshape(ROWS, KV_HEADS, share, HD)
    keys_all = key_cache.astype(jnp.float32).reshape(ROWS, CACHE_LEN, KV_HEADS, HD)
    values_all = value_cache.astype(jnp.float32).reshape(ROWS, CACHE_LEN, KV_HEADS, HD)
    key_own = new_key.astype(jnp.float32).reshape(ROWS, KV_HEADS, HD)
    value_own = new_value.astype(jnp.float32).reshape(ROWS, KV_HEADS, HD)
    scores = jnp.einsum('rkgd,rtkd->rkgt', q_heads, keys_all) * scale_factor
    valid = (jnp.arange(CACHE_LEN, dtype=jnp.int32)[None, :] < lengths[:, None])[:, None, None, :]
    scores = jnp.where(valid, scores, -jnp.inf)
    own_score = jnp.einsum('rkgd,rkd->rkg', q_heads, key_own) * scale_factor
    highest = jnp.maximum(lax.optimization_barrier(jnp.max(scores, axis=-1)), own_score)
    weights = jnp.exp(scores - highest[..., None])
    own_weight = jnp.exp(own_score - highest)
    total = lax.optimization_barrier(jnp.sum(weights, axis=-1)) + own_weight
    probs = (weights / total[..., None]).astype(jnp.bfloat16)
    own_prob = (own_weight / total).astype(jnp.bfloat16)
    heads_out = jnp.einsum('rkgt,rtkd->rkgd', probs.astype(jnp.float32), values_all)
    heads_out = heads_out + own_prob.astype(jnp.float32)[..., None] * value_own[:, :, None, :]
    attended = heads_out.reshape(ROWS, HEADS * HD).astype(jnp.bfloat16)
    projected = jnp.dot(attended, out_weight, preferred_element_type=jnp.float32)
    hidden_state = residual.astype(jnp.float32) + projected
    squares = lax.optimization_barrier(jnp.sum(hidden_state * hidden_state, axis=1))
    inv_rms = lax.rsqrt(squares / D + eps)
    scaled = hidden_state * norm_gain
    logits = jnp.dot(scaled, router_weight, precision=lax.Precision.HIGHEST) * inv_rms[:, None]
    normed = (scaled * inv_rms[:, None]).astype(jnp.bfloat16)
    chosen = jnp.take_along_axis(logits, expert_ids, axis=1)
    gates = jax.nn.softmax(chosen, axis=1)
    mixture = jnp.zeros((ROWS, D), jnp.float32)
    for expert in range(EXPERTS):
        low = expert * FF
        gate_part = jnp.dot(normed, gate_weight[:, low:low + FF], preferred_element_type=jnp.float32)
        up_part = jnp.dot(normed, up_weight[:, low:low + FF], preferred_element_type=jnp.float32)
        inner = (jax.nn.silu(gate_part) * up_part).astype(jnp.bfloat16)
        expert_out = jnp.dot(inner, down_weight[low:low + FF], preferred_element_type=jnp.float32)
        weight_row = lax.optimization_barrier(jnp.sum(gates * (expert_ids == expert).astype(jnp.float32), axis=1))
        mixture = mixture + weight_row[:, None] * expert_out
    return (hidden_state + mixture).astype(jnp.bfloat16)
```

```python
import functools

import jax
import jax.numpy as jnp
from jax import lax
from jax.experimental import pallas as pl
from jax.experimental.pallas import tpu as pltpu
from jax.sharding import PartitionSpec as P

D = 6144
HD = 128
EXPERTS = 4


eps = 1e-05


def attend(query, key_cache, value_cache, new_key, new_value, lengths):
    row_count = query.shape[0]
    slot_count = key_cache.shape[1]
    kv_local = key_cache.shape[2] // HD
    share = query.shape[1] // HD // kv_local
    scale_factor = HD ** (-0.5)
    q_heads = query.reshape(row_count, kv_local, share, HD)
    keys_all = key_cache.reshape(row_count, slot_count, kv_local, HD)
    values_all = value_cache.reshape(row_count, slot_count, kv_local, HD)
    key_own = new_key.reshape(row_count, kv_local, HD)
    value_own = new_value.reshape(row_count, kv_local, HD)
    scores = (
        jnp.einsum("rkgd,rtkd->rkgt", q_heads, keys_all, preferred_element_type=jnp.float32)
        * scale_factor
    )
    valid = (jnp.arange(slot_count, dtype=jnp.int32)[None, :] < lengths[:, None])[:, None, None, :]
    scores = jnp.where(valid, scores, -jnp.inf)
    own_score = (
        jnp.einsum("rkgd,rkd->rkg", q_heads, key_own, preferred_element_type=jnp.float32)
        * scale_factor
    )
    highest = jnp.maximum(jnp.max(scores, axis=-1), own_score)
    weights = jnp.exp(scores - highest[..., None])
    own_weight = jnp.exp(own_score - highest)
    total = jnp.sum(weights, axis=-1) + own_weight
    probs = (weights / total[..., None]).astype(jnp.bfloat16)
    own_prob = (own_weight / total).astype(jnp.bfloat16)
    heads_out = jnp.einsum("rkgt,rtkd->rkgd", probs, values_all, preferred_element_type=jnp.float32)
    heads_out = (
        heads_out
        + own_prob.astype(jnp.float32)[..., None] * value_own.astype(jnp.float32)[:, :, None, :]
    )
    return heads_out.reshape(row_count, kv_local * share * HD).astype(jnp.bfloat16)


def expert_block(rows_in, gate_weight, up_weight, down_weight):
    gate_part = jnp.dot(rows_in, gate_weight, preferred_element_type=jnp.float32)
    up_part = jnp.dot(rows_in, up_weight, preferred_element_type=jnp.float32)
    inner = (jax.nn.silu(gate_part) * up_part).astype(jnp.bfloat16)
    return jnp.dot(inner, down_weight, preferred_element_type=jnp.float32)


def shards(
    residual,
    query,
    key_cache,
    value_cache,
    new_key,
    new_value,
    lengths,
    out_weight,
    router_weight,
    norm_gain,
    expert_ids,
    gate_weight,
    up_weight,
    down_weight,
):
    attended = attend(query, key_cache, value_cache, new_key, new_value, lengths)
    partial_out = jnp.dot(
        lax.all_gather(attended, "units", axis=0, tiled=True),
        out_weight,
        preferred_element_type=jnp.float32,
    )
    projected = lax.psum(partial_out, "cuts")
    hidden_state = residual.astype(jnp.float32) + projected
    scaled = hidden_state * norm_gain
    local_squares = jnp.sum(hidden_state * hidden_state, axis=1)
    local_logits = jnp.dot(scaled, router_weight, precision=lax.Precision.HIGHEST)
    squares, logits_raw = lax.psum((local_squares, local_logits), "units")
    inv_rms = lax.rsqrt(squares / D + eps)
    logits = logits_raw * inv_rms[:, None]
    normed = (scaled * inv_rms[:, None]).astype(jnp.bfloat16)
    expert_range = jnp.arange(EXPERTS, dtype=jnp.int32)
    picked = (expert_ids[:, :, None] == expert_range[None, None, :]).astype(jnp.float32)
    chosen = jnp.sum(logits[:, None, :] * picked, axis=-1)
    gates = jax.nn.softmax(chosen, axis=1)
    per_expert = lax.axis_size("units") // EXPERTS
    expert_here = lax.axis_index("units") // per_expert
    weight_row = jnp.sum(gates * (expert_ids == expert_here).astype(jnp.float32), axis=1)
    rows_in = lax.all_gather(normed, "units", axis=1, tiled=True)
    expert_out = expert_block(rows_in, gate_weight, up_weight, down_weight)
    contribution = weight_row[:, None] * expert_out
    spread = lax.psum_scatter(
        contribution.astype(jnp.bfloat16), "units", scatter_dimension=1, tiled=True
    )
    mixture = lax.psum(spread, "cuts").astype(jnp.float32)
    return (hidden_state + mixture).astype(jnp.bfloat16)


F32 = jnp.float32
BF16 = jnp.bfloat16
W_SLOTS = 6
D_SLOTS = 4
PLANES = 4
CORES = 2
CUTS = 2


def partner(z, j):
    if j == 0:
        return z
    if j == 1:
        return z + 1 - 2 * lax.rem(z, 2)
    if j == 2:
        return lax.rem(z + 2, 4)
    return 3 - z


def dot(a, b, dims=((1,), (0,)), precision=None):
    return lax.dot_general(a, b, (dims, ((), ())), precision=precision, preferred_element_type=F32)


def layer_kernel(
    att, residual, gain, router_t, ids, ids_t, out_w, gate_w, up_w, down_w,
    out,
    wo, wg, wu, wd, a, psend, precv, hid, xs, x_in, accg, accu, inner, yf,
    ycs, ycr, yxs, yxr, yzs, yzr, fin, ssend, srecv,
    sem_o, sem_g, sem_u, sem_d,
    gz_s, gz_r, gc_s, gc_r, p_s, p_r, dz_s, dz_r, dx_s, dx_r, dc_s, dc_r,
    st_s, st_r, yc_s, yc_r, yx_s, yx_r, yz_s, yz_r, f_s, f_r,
):
    g, u, x = lax.axis_index("groups"), lax.axis_index("units"), lax.axis_index("cuts")
    z, c = u // CORES, lax.rem(u, CORES)
    rows = a.shape[0]
    row_block = att.shape[0]
    block = wd.shape[2]
    half = block // CUTS
    cap = x_in.shape[0]
    units = PLANES * CORES
    count = units * CUTS
    me = u * CUTS + x
    ox, oc = 1 - x, 1 - c
    pending = []

    def unit(plane, core):
        return plane * CORES + core

    def remote(src, dst, ss, rs, to_unit, to_cut):
        return pltpu.make_async_remote_copy(
            src_ref=src, dst_ref=dst, send_sem=ss, recv_sem=rs,
            device_id=(g, to_unit, to_cut), device_id_type=pl.DeviceIdType.MESH,
        )

    def send(*args):
        copy = remote(*args)
        copy.start()
        pending.append(copy)
        return copy

    copy_o = pltpu.make_async_copy(out_w, wo, sem_o)
    copy_o.start()

    barrier = pltpu.get_barrier_semaphore()
    for k in range(1, count):
        t = lax.rem(me + k, count)
        pl.semaphore_signal(barrier, inc=1, device_id=(g, t // CUTS, lax.rem(t, CUTS)), device_id_type=pl.DeviceIdType.MESH)

    def cols_of(index):
        return pl.ds(pl.multiple_of(index * block, 128), block)

    chunks = [(j, own) for j in range(PLANES) for own in (True, False)]

    def chunk_unit(k):
        j, own = chunks[k]
        return unit(partner(z, j), c if own else oc)

    def weight_copies(k):
        slot = k % W_SLOTS
        part = pl.ds(pl.multiple_of(chunk_unit(k) * block, 128), block)
        return (
            pltpu.make_async_copy(gate_w.at[part, :], wg.at[slot], sem_g.at[slot]),
            pltpu.make_async_copy(up_w.at[part, :], wu.at[slot], sem_u.at[slot]),
        )

    def start_weights(k):
        for copy in weight_copies(k):
            copy.start()

    d_chunks = [(j, own) for j in (3, 2, 1, 0) for own in (False, True)]

    def down_copy(k):
        j, own = d_chunks[k]
        slot = k % D_SLOTS
        return pltpu.make_async_copy(down_w.at[:, cols_of(unit(partner(z, j), c if own else oc))], wd.at[slot], sem_d.at[slot])

    def rows_of(index):
        return pl.ds(pl.multiple_of(index * row_block, 16), row_block)

    a[rows_of(u), :] = att[...]
    pl.semaphore_wait(barrier, count - 1)
    mine = a.at[rows_of(u), :]
    for j in (3, 2, 1):
        send(mine, mine, gz_s.at[j], gz_r.at[j], unit(partner(z, j), c), x)
    send(mine, mine, gc_s.at[0], gc_r.at[0], unit(z, oc), x)

    copy_o.wait()
    for k in range(W_SLOTS):
        start_weights(k)
    for k in range(D_SLOTS):
        down_copy(k).start()

    ids_row = ids_t[...]
    e_iota = lax.broadcasted_iota(jnp.int32, (8, rows), 0)
    named_t = (ids_row[0:1, :] == e_iota) | (ids_row[1:2, :] == e_iota)
    r0 = lax.broadcasted_iota(jnp.int32, (rows, rows), 0)
    r1 = lax.broadcasted_iota(jnp.int32, (rows, rows), 1)
    upper = jnp.where(r0 <= r1, 1.0, 0.0)
    place_t = dot(jnp.where(named_t, 1.0, 0.0), upper)
    place_t = jnp.where(named_t, place_t, 0.0)
    s_iota = (lax.broadcasted_iota(jnp.int32, (cap, rows), 0) + 1).astype(F32)

    def pick(row):
        return jnp.where(row == s_iota, 1.0, 0.0)

    for j in (1, 2, 3):
        there = unit(partner(z, j), c)
        got = a.at[rows_of(there), :]
        remote(got, got, gz_s.at[j], gz_r.at[j], there, x).wait_recv()
        send(got, got, gc_s.at[j], gc_r.at[j], unit(z, oc), x)
    for j in range(PLANES):
        got = a.at[rows_of(unit(partner(z, j), oc)), :]
        remote(got, got, gc_s.at[j], gc_r.at[j], unit(z, oc), x).wait_recv()

    def half_of(index):
        return pl.ds(pl.multiple_of(index * half, 128), half)

    psend[...] = dot(a[...], wo[:, half_of(ox)]).astype(BF16)
    psum_copy = send(psend, precv, p_s, p_r, u, ox)
    own_part = dot(a[...], wo[:, half_of(x)])
    own_part = own_part + residual[:, half_of(x)].astype(F32)
    psum_copy.wait_recv()
    hidden = own_part + precv[...].astype(F32)
    hid[...] = hidden
    scaled = hidden * gain[:, half_of(x)]
    scaled16 = scaled.astype(BF16)

    def line_cols(plane, core, cut):
        return pl.ds(pl.multiple_of(unit(plane, core) * block + cut * half, 128), half)

    def place_row(expert):
        return jnp.sum(jnp.where(e_iota == expert, place_t, 0.0), axis=0, keepdims=True)

    for j in (3, 2, 1):
        to = partner(z, j)
        xs[j] = dot(pick(place_row(to)).astype(BF16), scaled16).astype(BF16)
        send(xs.at[j], x_in.at[:, line_cols(z, c, x)], dz_s.at[j], dz_r.at[j], unit(to, c), x)
    my_pick = pick(place_row(z))
    x_in[:, line_cols(z, c, x)] = dot(my_pick.astype(BF16), scaled16).astype(BF16)

    def spread(j):
        plane = partner(z, j)
        got = x_in.at[:, line_cols(plane, c, x)]
        if j:
            remote(got, got, dz_s.at[j], dz_r.at[j], unit(plane, c), x).wait_recv()
        send(got, got, dx_s.at[j], dx_r.at[j], u, ox)
        send(got, got, dc_s.at[2 * j], dc_r.at[2 * j], unit(z, oc), x)

    def relay(j):
        got = x_in.at[:, line_cols(partner(z, j), c, ox)]
        remote(got, got, dx_s.at[j], dx_r.at[j], u, ox).wait_recv()
        send(got, got, dc_s.at[2 * j + 1], dc_r.at[2 * j + 1], unit(z, oc), x)

    spread(0)
    high = lax.Precision.HIGHEST
    sq = dot(jnp.ones((8, half), F32), hidden * hidden, ((1,), (1,)), high)
    lg = dot(router_t[:, half_of(x)], scaled, ((1,), (1,)), high)
    stat = jnp.where(e_iota == 4, sq, lg)
    ssend[...] = stat
    for k in range(1, count):
        t = lax.rem(me + k, count)
        send(ssend, srecv.at[me], st_s.at[k], st_r.at[me], t // CUTS, lax.rem(t, CUTS))

    def feed(k):
        j, own = chunks[k]
        if not own:
            for i in (0, 1):
                got = x_in.at[:, line_cols(partner(z, j), oc, x if i == 0 else ox)]
                remote(got, got, dc_s.at[2 * j + i], dc_r.at[2 * j + i], unit(z, oc), x).wait_recv()
        for copy in weight_copies(k):
            copy.wait()
        slot = k % W_SLOTS
        tile = 512

        @pl.loop(0, wg.shape[2] // tile)
        def _(i):
            cols = pl.ds(pl.multiple_of(i * tile, 128), tile)
            rows_x = x_in[:, cols_of(chunk_unit(k))]
            part_g = dot(rows_x, wg[slot, :, cols])
            part_u = dot(rows_x, wu[slot, :, cols])
            if k == 0:
                accg[:, cols] = part_g
                accu[:, cols] = part_u
            else:
                accg[:, cols] += part_g
                accu[:, cols] += part_u

        if k + W_SLOTS < len(chunks):
            start_weights(k + W_SLOTS)

    spread(1)
    relay(0)
    feed(0)
    spread(2)
    relay(1)
    feed(1)
    spread(3)
    relay(2)
    feed(2)
    relay(3)
    for k in range(3, len(chunks)):
        feed(k)

    total = stat
    for k in range(1, count):
        t = lax.rem(me + k, count)
        remote(ssend, srecv.at[t], st_s.at[k], st_r.at[t], t // CUTS, lax.rem(t, CUTS)).wait_recv()
        total = total + srecv[t]
    inv = lax.rsqrt(jnp.sum(jnp.where(e_iota == 4, total, 0.0), axis=0, keepdims=True) / D + eps)
    inv_col = jnp.sum(my_pick * inv, axis=1, keepdims=True)
    tile = 512

    @pl.loop(0, inner.shape[1] // tile)
    def _(i):
        cols = pl.ds(pl.multiple_of(i * tile, 128), tile)
        gate_part = accg[:, cols] * inv_col
        up_part = accu[:, cols] * inv_col
        inner[:, cols] = (gate_part * jax.nn.sigmoid(gate_part) * up_part).astype(BF16)

    def down_part(k):
        down_copy(k).wait()
        slot = k % D_SLOTS
        tile = 256

        @pl.loop(0, block // tile)
        def _(i):
            cols = pl.ds(pl.multiple_of(i * tile, 128), tile)
            yf[:, cols] = dot(inner[...], wd[slot, :, cols])

        if k + D_SLOTS < len(d_chunks):
            down_copy(k + D_SLOTS).start()

    def finish(j):
        remote(yxs.at[j], yxr.at[j], yx_s.at[j], yx_r.at[j], u, ox).wait_recv()
        yzs[j] = (hid_y[j] + yxr[j].astype(F32)).astype(BF16)
        if j:
            send(yzs.at[j], yzr.at[j], yz_s.at[j], yz_r.at[j], unit(partner(z, j), c), x)

    hid_y = {}
    order = (3, 2, 1, 0)
    for n, j in enumerate(order):
        down_part(2 * n)
        ycs[j] = yf[...].astype(BF16)
        core_copy = send(ycs.at[j], ycr.at[j], yc_s.at[j], yc_r.at[j], unit(z, oc), x)
        down_part(2 * n + 1)
        if n:
            finish(order[n - 1])
        core_copy.wait_recv()
        yf[...] = yf[...] + ycr[j].astype(F32)
        yxs[j] = yf[:, half_of(ox)].astype(BF16)
        send(yxs.at[j], yxr.at[j], yx_s.at[j], yx_r.at[j], u, ox)
        hid_y[j] = yf[:, half_of(x)]

    lane = lax.broadcasted_iota(jnp.int32, (rows, rows), 1)
    ids_col = ids[...]
    named = (ids_col[:, 0:1] == lane) | (ids_col[:, 1:2] == lane)
    lower = jnp.where(r1 <= r0, 1.0, 0.0)
    place = jnp.where(named, dot(lower, jnp.where(named, 1.0, 0.0)), 0.0)
    logits = total * inv
    top = jnp.max(jnp.where(named_t, logits, -jnp.inf), axis=0, keepdims=True)
    raised = jnp.where(named_t, jnp.exp(jnp.where(named_t, logits - top, 0.0)), 0.0)
    gates = raised / jnp.sum(raised, axis=0, keepdims=True)
    spot = (lax.broadcasted_iota(jnp.int32, (rows, cap), 1) + 1).astype(F32)

    def share_of(expert, contribution):
        weight = jnp.sum(jnp.where(r0 == r1, jnp.sum(jnp.where(e_iota == expert, gates, 0.0), axis=0, keepdims=True), 0.0), axis=1, keepdims=True)
        column = jnp.sum(jnp.where(lane == expert, place, 0.0), axis=1, keepdims=True)
        return weight * dot(jnp.where(column == spot, 1.0, 0.0).astype(BF16), contribution)

    mixed = hid[...]
    for j in (1, 2, 3):
        if j == 3:
            finish(0)
            mixed = mixed + share_of(z, yzs[0])
        plane = partner(z, j)
        remote(yzs.at[j], yzr.at[j], yz_s.at[j], yz_r.at[j], unit(plane, c), x).wait_recv()
        mixed = mixed + share_of(plane, yzr[j])
    done = mixed.astype(BF16)
    fin[0] = done
    last = send(fin.at[0], fin.at[1], f_s, f_r, u, ox)
    out[:, half_of(x)] = done
    last.wait_recv()
    out[:, half_of(ox)] = fin[1]
    for copy in pending:
        copy.wait_send()


def layer(att, residual, gain, router_t, ids, ids_t, out_w, gate_w, up_w, down_w):
    rows = residual.shape[0]
    block = residual.shape[1]
    half = block // CUTS
    cap = rows * 5 // 8
    hidden_units = gate_w.shape[1]
    count = PLANES * CORES * CUTS
    vmem = pl.BlockSpec(memory_space=pltpu.VMEM)
    hbm = pl.BlockSpec(memory_space=pl.ANY)
    dma = pltpu.SemaphoreType.DMA
    return pl.pallas_call(
        layer_kernel,
        out_shape=jax.ShapeDtypeStruct((rows, block), BF16),
        in_specs=[vmem] * 6 + [hbm] * 4,
        out_specs=vmem,
        scratch_shapes=[
            pltpu.VMEM(out_w.shape, BF16),
            pltpu.VMEM((W_SLOTS, block, hidden_units), BF16),
            pltpu.VMEM((W_SLOTS, block, hidden_units), BF16),
            pltpu.VMEM((D_SLOTS, hidden_units, block), BF16),
            pltpu.VMEM((rows, att.shape[1]), BF16),
            pltpu.VMEM((rows, half), BF16),
            pltpu.VMEM((rows, half), BF16),
            pltpu.VMEM((rows, half), F32),
            pltpu.VMEM((PLANES, cap, half), BF16),
            pltpu.VMEM((cap, D), BF16),
            pltpu.VMEM((cap, hidden_units), F32),
            pltpu.VMEM((cap, hidden_units), F32),
            pltpu.VMEM((cap, hidden_units), BF16),
            pltpu.VMEM((cap, block), F32),
            pltpu.VMEM((PLANES, cap, block), BF16),
            pltpu.VMEM((PLANES, cap, block), BF16),
            pltpu.VMEM((PLANES, cap, half), BF16),
            pltpu.VMEM((PLANES, cap, half), BF16),
            pltpu.VMEM((PLANES, cap, half), BF16),
            pltpu.VMEM((PLANES, cap, half), BF16),
            pltpu.VMEM((2, rows, half), BF16),
            pltpu.VMEM((8, rows), F32),
            pltpu.VMEM((count, 8, rows), F32),
            dma(()), dma((W_SLOTS,)), dma((W_SLOTS,)), dma((D_SLOTS,)),
            dma((4,)), dma((4,)), dma((4,)), dma((4,)), dma(()), dma(()),
            dma((4,)), dma((4,)), dma((4,)), dma((4,)), dma((8,)), dma((8,)),
            dma((count,)), dma((count,)),
            dma((4,)), dma((4,)), dma((4,)), dma((4,)), dma((4,)), dma((4,)),
            dma(()), dma(()),
        ],
        compiler_params=pltpu.CompilerParams(
            collective_id=0, has_side_effects=True, vmem_limit_bytes=VMEM_MIB * 2**20
        ),
        name="layer",
    )(att, residual, gain, router_t, ids, ids_t, out_w, gate_w, up_w, down_w)


VMEM_MIB = 62


def fused_shards(
    residual, query, key_cache, value_cache, new_key, new_value, lengths, out_weight,
    router_weight, norm_gain, expert_ids, gate_weight, up_weight, down_weight,
):
    attended = attend(query, key_cache, value_cache, new_key, new_value, lengths)
    router_t = jnp.pad(router_weight.T, ((0, 8 - EXPERTS), (0, 0)))
    return layer(
        attended, residual, norm_gain[None, :], router_t, expert_ids, expert_ids.T,
        out_weight, gate_weight, up_weight, down_weight,
    )


def solution(mesh):
    placed = (
        P("groups", "units"),
        P(("groups", "units"), "cuts"),
        P(("groups", "units"), None, "cuts"),
        P(("groups", "units"), None, "cuts"),
        P(("groups", "units"), "cuts"),
        P(("groups", "units"), "cuts"),
        P(("groups", "units")),
        P("cuts", "units"),
        P("units", None),
        P("units"),
        P("groups", None),
        P(None, ("units", "cuts")),
        P(None, ("units", "cuts")),
        P(("units", "cuts"), None),
    )
    fits = (mesh.shape["units"], mesh.shape["cuts"]) == (PLANES * CORES, CUTS)
    return jax.shard_map(
        fused_shards if fits else shards, mesh=mesh, in_specs=placed, out_specs=P("groups", "units"), check_vma=False
    )
```

```python
import functools

import jax
import jax.numpy as jnp
from jax import lax
from jax.experimental import pallas as pl
from jax.experimental.pallas import tpu as pltpu
from jax.sharding import PartitionSpec as P

D = 6144
HD = 128
EXPERTS = 4


eps = 1e-05


def attend(query, key_cache, value_cache, new_key, new_value, lengths):
    row_count = query.shape[0]
    slot_count = key_cache.shape[1]
    kv_local = key_cache.shape[2] // HD
    share = query.shape[1] // HD // kv_local
    scale_factor = HD ** (-0.5)
    q_heads = query.reshape(row_count, kv_local, share, HD)
    keys_all = key_cache.reshape(row_count, slot_count, kv_local, HD)
    values_all = value_cache.reshape(row_count, slot_count, kv_local, HD)
    key_own = new_key.reshape(row_count, kv_local, HD)
    value_own = new_value.reshape(row_count, kv_local, HD)
    scores = (
        jnp.einsum("rkgd,rtkd->rkgt", q_heads, keys_all, preferred_element_type=jnp.float32)
        * scale_factor
    )
    valid = (jnp.arange(slot_count, dtype=jnp.int32)[None, :] < lengths[:, None])[:, None, None, :]
    scores = jnp.where(valid, scores, -jnp.inf)
    own_score = (
        jnp.einsum("rkgd,rkd->rkg", q_heads, key_own, preferred_element_type=jnp.float32)
        * scale_factor
    )
    highest = jnp.maximum(jnp.max(scores, axis=-1), own_score)
    weights = jnp.exp(scores - highest[..., None])
    own_weight = jnp.exp(own_score - highest)
    total = jnp.sum(weights, axis=-1) + own_weight
    probs = (weights / total[..., None]).astype(jnp.bfloat16)
    own_prob = (own_weight / total).astype(jnp.bfloat16)
    heads_out = jnp.einsum("rkgt,rtkd->rkgd", probs, values_all, preferred_element_type=jnp.float32)
    heads_out = (
        heads_out
        + own_prob.astype(jnp.float32)[..., None] * value_own.astype(jnp.float32)[:, :, None, :]
    )
    return heads_out.reshape(row_count, kv_local * share * HD).astype(jnp.bfloat16)


def expert_block(rows_in, gate_weight, up_weight, down_weight):
    gate_part = jnp.dot(rows_in, gate_weight, preferred_element_type=jnp.float32)
    up_part = jnp.dot(rows_in, up_weight, preferred_element_type=jnp.float32)
    inner = (jax.nn.silu(gate_part) * up_part).astype(jnp.bfloat16)
    return jnp.dot(inner, down_weight, preferred_element_type=jnp.float32)


def shards(
    residual,
    query,
    key_cache,
    value_cache,
    new_key,
    new_value,
    lengths,
    out_weight,
    router_weight,
    norm_gain,
    expert_ids,
    gate_weight,
    up_weight,
    down_weight,
):
    attended = attend(query, key_cache, value_cache, new_key, new_value, lengths)
    partial_out = jnp.dot(
        lax.all_gather(attended, "units", axis=0, tiled=True),
        out_weight,
        preferred_element_type=jnp.float32,
    )
    projected = lax.psum(partial_out, "cuts")
    hidden_state = residual.astype(jnp.float32) + projected
    scaled = hidden_state * norm_gain
    local_squares = jnp.sum(hidden_state * hidden_state, axis=1)
    local_logits = jnp.dot(scaled, router_weight, precision=lax.Precision.HIGHEST)
    squares, logits_raw = lax.psum((local_squares, local_logits), "units")
    inv_rms = lax.rsqrt(squares / D + eps)
    logits = logits_raw * inv_rms[:, None]
    normed = (scaled * inv_rms[:, None]).astype(jnp.bfloat16)
    expert_range = jnp.arange(EXPERTS, dtype=jnp.int32)
    picked = (expert_ids[:, :, None] == expert_range[None, None, :]).astype(jnp.float32)
    chosen = jnp.sum(logits[:, None, :] * picked, axis=-1)
    gates = jax.nn.softmax(chosen, axis=1)
    per_expert = lax.axis_size("units") // EXPERTS
    expert_here = lax.axis_index("units") // per_expert
    weight_row = jnp.sum(gates * (expert_ids == expert_here).astype(jnp.float32), axis=1)
    rows_in = lax.all_gather(normed, "units", axis=1, tiled=True)
    expert_out = expert_block(rows_in, gate_weight, up_weight, down_weight)
    contribution = weight_row[:, None] * expert_out
    spread = lax.psum_scatter(
        contribution.astype(jnp.bfloat16), "units", scatter_dimension=1, tiled=True
    )
    mixture = lax.psum(spread, "cuts").astype(jnp.float32)
    return (hidden_state + mixture).astype(jnp.bfloat16)


F32 = jnp.float32
BF16 = jnp.bfloat16
W_SLOTS = 6
D_SLOTS = 4
PLANES = 4
CORES = 2
CUTS = 2


def partner(z, j):
    if j == 0:
        return z
    if j == 1:
        return z + 1 - 2 * lax.rem(z, 2)
    if j == 2:
        return lax.rem(z + 2, 4)
    return 3 - z


def dot(a, b, dims=((1,), (0,)), precision=None):
    return lax.dot_general(a, b, (dims, ((), ())), precision=precision, preferred_element_type=F32)


def layer_kernel(
    query, new_key, new_value, lengths, residual, gain, router_t, ids, ids_t, key_cache, value_cache, out_w, gate_w, up_w, down_w,
    out,
    wo, wg, wu, wd, qs, os, nk, nv, a, psend, precv, hid, xs, x_in, accg, accu, inner, yf,
    ycs, ycr, yxs, yxr, yzs, yzr, fin, ssend, srecv,
    sem_o, sem_g, sem_u, sem_d, sem_kv,
    gz_s, gz_r, gc_s, gc_r, p_s, p_r, dz_s, dz_r, dx_s, dx_r, dc_s, dc_r,
    st_s, st_r, yc_s, yc_r, yx_s, yx_r, yz_s, yz_r, f_s, f_r,
):
    g, u, x = lax.axis_index("groups"), lax.axis_index("units"), lax.axis_index("cuts")
    z, c = u // CORES, lax.rem(u, CORES)
    rows = a.shape[0]
    row_block = query.shape[0]
    block = wd.shape[2]
    half = block // CUTS
    cap = x_in.shape[0]
    units = PLANES * CORES
    count = units * CUTS
    me = u * CUTS + x
    ox, oc = 1 - x, 1 - c
    pending = []

    def unit(plane, core):
        return plane * CORES + core

    def remote(src, dst, ss, rs, to_unit, to_cut):
        return pltpu.make_async_remote_copy(
            src_ref=src, dst_ref=dst, send_sem=ss, recv_sem=rs,
            device_id=(g, to_unit, to_cut), device_id_type=pl.DeviceIdType.MESH,
        )

    def send(*args):
        copy = remote(*args)
        copy.start()
        pending.append(copy)
        return copy

    slots, lanes = key_cache.shape[1], key_cache.shape[2]
    steps = row_block // 2

    def cache_copies(step, slot):
        for i in range(2):
            for n, cache in enumerate((key_cache, value_cache)):
                yield pltpu.make_async_copy(
                    cache.at[2 * step + i],
                    wd.at[slot, pl.ds((2 * i + n) * slots, slots), pl.ds(0, lanes)],
                    sem_kv.at[slot, 2 * i + n],
                )

    for step in range(D_SLOTS):
        for copy in cache_copies(step, step):
            copy.start()
    copy_o = pltpu.make_async_copy(out_w, wo, sem_o)
    copy_o.start()

    barrier = pltpu.get_barrier_semaphore()
    for k in range(1, count):
        t = lax.rem(me + k, count)
        pl.semaphore_signal(barrier, inc=1, device_id=(g, t // CUTS, lax.rem(t, CUTS)), device_id_type=pl.DeviceIdType.MESH)

    def cols_of(index):
        return pl.ds(pl.multiple_of(index * block, 128), block)

    chunks = [(j, own) for j in range(PLANES) for own in (True, False)]

    def chunk_unit(k):
        j, own = chunks[k]
        return unit(partner(z, j), c if own else oc)

    def weight_copies(k):
        slot = k % W_SLOTS
        part = pl.ds(pl.multiple_of(chunk_unit(k) * block, 128), block)
        return (
            pltpu.make_async_copy(gate_w.at[part, :], wg.at[slot], sem_g.at[slot]),
            pltpu.make_async_copy(up_w.at[part, :], wu.at[slot], sem_u.at[slot]),
        )

    def start_weights(k):
        for copy in weight_copies(k):
            copy.start()

    d_chunks = [(j, own) for j in (3, 2, 1, 0) for own in (False, True)]

    def down_copy(k):
        j, own = d_chunks[k]
        slot = k % D_SLOTS
        return pltpu.make_async_copy(down_w.at[:, cols_of(unit(partner(z, j), c if own else oc))], wd.at[slot], sem_d.at[slot])

    def rows_of(index):
        return pl.ds(pl.multiple_of(index * row_block, 16), row_block)

    heads = query.shape[1] // HD
    kv_heads = lanes // HD
    share = heads // kv_heads
    qs[...] = query[...].astype(F32).reshape(row_block, heads, HD)
    own_head = (
        lax.broadcasted_iota(jnp.int32, (heads, lanes), 0) // share
        == lax.broadcasted_iota(jnp.int32, (heads, lanes), 1) // HD
    )
    slot_iota = lax.broadcasted_iota(jnp.int32, (heads, slots), 1)

    def attend_step(step, slot):
        for copy in cache_copies(step, slot):
            copy.wait()
        for i in range(2):
            row = 2 * step + i
            q = jnp.where(own_head, jnp.concatenate([qs[row]] * kv_heads, axis=1), 0.0)
            keys = wd[slot, pl.ds(2 * i * slots, slots), pl.ds(0, lanes)]
            values = wd[slot, pl.ds((2 * i + 1) * slots, slots), pl.ds(0, lanes)]
            scores = dot(q.astype(BF16), keys, ((1,), (1,))) * HD ** (-0.5)
            own = jnp.sum(q * nk[pl.ds(row, 1), :], axis=1, keepdims=True) * HD ** (-0.5)
            valid = slot_iota < lengths[row]
            highest = jnp.maximum(jnp.max(jnp.where(valid, scores, -jnp.inf), axis=1, keepdims=True), own)
            weights = jnp.where(valid, jnp.exp(jnp.where(valid, scores - highest, 0.0)), 0.0)
            own_weight = jnp.exp(own - highest)
            all_weight = jnp.sum(weights, axis=1, keepdims=True) + own_weight
            probs = (weights / all_weight).astype(BF16)
            own_prob = (own_weight / all_weight).astype(BF16).astype(F32)
            mix = dot(probs, values) + own_prob * nv[pl.ds(row, 1), :]
            mix = jnp.where(own_head, mix, 0.0)
            heads_out = mix[:, :HD]
            for n in range(1, kv_heads):
                heads_out = heads_out + mix[:, n * HD:(n + 1) * HD]
            os[row] = heads_out

    nk[...] = new_key[...].astype(F32)
    nv[...] = new_value[...].astype(F32)

    @pl.loop(0, steps - D_SLOTS)
    def _(step):
        slot = lax.rem(step, D_SLOTS)
        attend_step(step, slot)
        for copy in cache_copies(step + D_SLOTS, slot):
            copy.start()

    for k in range(W_SLOTS):
        start_weights(k)

    @pl.loop(steps - D_SLOTS, steps)
    def _(step):
        attend_step(step, lax.rem(step, D_SLOTS))

    for k in range(D_SLOTS):
        down_copy(k).start()
    a[rows_of(u), :] = os[...].reshape(row_block, heads * HD).astype(BF16)
    pl.semaphore_wait(barrier, count - 1)
    mine = a.at[rows_of(u), :]
    for j in (3, 2, 1):
        send(mine, mine, gz_s.at[j], gz_r.at[j], unit(partner(z, j), c), x)
    send(mine, mine, gc_s.at[0], gc_r.at[0], unit(z, oc), x)

    copy_o.wait()

    ids_row = ids_t[...]
    e_iota = lax.broadcasted_iota(jnp.int32, (8, rows), 0)
    named_t = (ids_row[0:1, :] == e_iota) | (ids_row[1:2, :] == e_iota)
    r0 = lax.broadcasted_iota(jnp.int32, (rows, rows), 0)
    r1 = lax.broadcasted_iota(jnp.int32, (rows, rows), 1)
    upper = jnp.where(r0 <= r1, 1.0, 0.0)
    place_t = dot(jnp.where(named_t, 1.0, 0.0), upper)
    place_t = jnp.where(named_t, place_t, 0.0)
    s_iota = (lax.broadcasted_iota(jnp.int32, (cap, rows), 0) + 1).astype(F32)

    def pick(row):
        return jnp.where(row == s_iota, 1.0, 0.0)

    for j in (1, 2, 3):
        there = unit(partner(z, j), c)
        got = a.at[rows_of(there), :]
        remote(got, got, gz_s.at[j], gz_r.at[j], there, x).wait_recv()
        send(got, got, gc_s.at[j], gc_r.at[j], unit(z, oc), x)
    for j in range(PLANES):
        got = a.at[rows_of(unit(partner(z, j), oc)), :]
        remote(got, got, gc_s.at[j], gc_r.at[j], unit(z, oc), x).wait_recv()

    def half_of(index):
        return pl.ds(pl.multiple_of(index * half, 128), half)

    psend[...] = dot(a[...], wo[:, half_of(ox)]).astype(BF16)
    psum_copy = send(psend, precv, p_s, p_r, u, ox)
    own_part = dot(a[...], wo[:, half_of(x)])
    own_part = own_part + residual[:, half_of(x)].astype(F32)
    psum_copy.wait_recv()
    hidden = own_part + precv[...].astype(F32)
    hid[...] = hidden
    scaled = hidden * gain[:, half_of(x)]
    scaled16 = scaled.astype(BF16)

    def line_cols(plane, core, cut):
        return pl.ds(pl.multiple_of(unit(plane, core) * block + cut * half, 128), half)

    def place_row(expert):
        return jnp.sum(jnp.where(e_iota == expert, place_t, 0.0), axis=0, keepdims=True)

    for j in (3, 2, 1):
        to = partner(z, j)
        xs[j] = dot(pick(place_row(to)).astype(BF16), scaled16).astype(BF16)
        send(xs.at[j], x_in.at[:, line_cols(z, c, x)], dz_s.at[j], dz_r.at[j], unit(to, c), x)
    my_pick = pick(place_row(z))
    x_in[:, line_cols(z, c, x)] = dot(my_pick.astype(BF16), scaled16).astype(BF16)

    def spread(j):
        plane = partner(z, j)
        got = x_in.at[:, line_cols(plane, c, x)]
        if j:
            remote(got, got, dz_s.at[j], dz_r.at[j], unit(plane, c), x).wait_recv()
        send(got, got, dx_s.at[j], dx_r.at[j], u, ox)
        send(got, got, dc_s.at[2 * j], dc_r.at[2 * j], unit(z, oc), x)

    def relay(j):
        got = x_in.at[:, line_cols(partner(z, j), c, ox)]
        remote(got, got, dx_s.at[j], dx_r.at[j], u, ox).wait_recv()
        send(got, got, dc_s.at[2 * j + 1], dc_r.at[2 * j + 1], unit(z, oc), x)

    spread(0)
    high = lax.Precision.HIGHEST
    sq = dot(jnp.ones((8, half), F32), hidden * hidden, ((1,), (1,)), high)
    lg = dot(router_t[:, half_of(x)], scaled, ((1,), (1,)), high)
    stat = jnp.where(e_iota == 4, sq, lg)
    ssend[...] = stat
    for k in range(1, count):
        t = lax.rem(me + k, count)
        send(ssend, srecv.at[me], st_s.at[k], st_r.at[me], t // CUTS, lax.rem(t, CUTS))

    def feed(k):
        j, own = chunks[k]
        if not own:
            for i in (0, 1):
                got = x_in.at[:, line_cols(partner(z, j), oc, x if i == 0 else ox)]
                remote(got, got, dc_s.at[2 * j + i], dc_r.at[2 * j + i], unit(z, oc), x).wait_recv()
        for copy in weight_copies(k):
            copy.wait()
        slot = k % W_SLOTS
        tile = 512

        @pl.loop(0, wg.shape[2] // tile)
        def _(i):
            cols = pl.ds(pl.multiple_of(i * tile, 128), tile)
            rows_x = x_in[:, cols_of(chunk_unit(k))]
            part_g = dot(rows_x, wg[slot, :, cols])
            part_u = dot(rows_x, wu[slot, :, cols])
            if k == 0:
                accg[:, cols] = part_g
                accu[:, cols] = part_u
            else:
                accg[:, cols] += part_g
                accu[:, cols] += part_u

        if k + W_SLOTS < len(chunks):
            start_weights(k + W_SLOTS)

    spread(1)
    relay(0)
    feed(0)
    spread(2)
    relay(1)
    feed(1)
    spread(3)
    relay(2)
    feed(2)
    relay(3)
    for k in range(3, len(chunks)):
        feed(k)

    total = stat
    for k in range(1, count):
        t = lax.rem(me + k, count)
        remote(ssend, srecv.at[t], st_s.at[k], st_r.at[t], t // CUTS, lax.rem(t, CUTS)).wait_recv()
        total = total + srecv[t]
    inv = lax.rsqrt(jnp.sum(jnp.where(e_iota == 4, total, 0.0), axis=0, keepdims=True) / D + eps)
    inv_col = jnp.sum(my_pick * inv, axis=1, keepdims=True)
    tile = 512

    @pl.loop(0, inner.shape[1] // tile)
    def _(i):
        cols = pl.ds(pl.multiple_of(i * tile, 128), tile)
        gate_part = accg[:, cols] * inv_col
        up_part = accu[:, cols] * inv_col
        inner[:, cols] = (gate_part * jax.nn.sigmoid(gate_part) * up_part).astype(BF16)

    def down_part(k):
        down_copy(k).wait()
        slot = k % D_SLOTS
        tile = 256

        @pl.loop(0, block // tile)
        def _(i):
            cols = pl.ds(pl.multiple_of(i * tile, 128), tile)
            yf[:, cols] = dot(inner[...], wd[slot, :, cols])

        if k + D_SLOTS < len(d_chunks):
            down_copy(k + D_SLOTS).start()

    def finish(j):
        remote(yxs.at[j], yxr.at[j], yx_s.at[j], yx_r.at[j], u, ox).wait_recv()
        yzs[j] = (hid_y[j] + yxr[j].astype(F32)).astype(BF16)
        if j:
            send(yzs.at[j], yzr.at[j], yz_s.at[j], yz_r.at[j], unit(partner(z, j), c), x)

    hid_y = {}
    order = (3, 2, 1, 0)
    for n, j in enumerate(order):
        down_part(2 * n)
        ycs[j] = yf[...].astype(BF16)
        core_copy = send(ycs.at[j], ycr.at[j], yc_s.at[j], yc_r.at[j], unit(z, oc), x)
        down_part(2 * n + 1)
        if n:
            finish(order[n - 1])
        core_copy.wait_recv()
        yf[...] = yf[...] + ycr[j].astype(F32)
        yxs[j] = yf[:, half_of(ox)].astype(BF16)
        send(yxs.at[j], yxr.at[j], yx_s.at[j], yx_r.at[j], u, ox)
        hid_y[j] = yf[:, half_of(x)]

    lane = lax.broadcasted_iota(jnp.int32, (rows, rows), 1)
    ids_col = ids[...]
    named = (ids_col[:, 0:1] == lane) | (ids_col[:, 1:2] == lane)
    lower = jnp.where(r1 <= r0, 1.0, 0.0)
    place = jnp.where(named, dot(lower, jnp.where(named, 1.0, 0.0)), 0.0)
    logits = total * inv
    top = jnp.max(jnp.where(named_t, logits, -jnp.inf), axis=0, keepdims=True)
    raised = jnp.where(named_t, jnp.exp(jnp.where(named_t, logits - top, 0.0)), 0.0)
    gates = raised / jnp.sum(raised, axis=0, keepdims=True)
    spot = (lax.broadcasted_iota(jnp.int32, (rows, cap), 1) + 1).astype(F32)

    def share_of(expert, contribution):
        weight = jnp.sum(jnp.where(r0 == r1, jnp.sum(jnp.where(e_iota == expert, gates, 0.0), axis=0, keepdims=True), 0.0), axis=1, keepdims=True)
        column = jnp.sum(jnp.where(lane == expert, place, 0.0), axis=1, keepdims=True)
        return weight * dot(jnp.where(column == spot, 1.0, 0.0).astype(BF16), contribution)

    mixed = hid[...]
    for j in (1, 2, 3):
        if j == 3:
            finish(0)
            mixed = mixed + share_of(z, yzs[0])
        plane = partner(z, j)
        remote(yzs.at[j], yzr.at[j], yz_s.at[j], yz_r.at[j], unit(plane, c), x).wait_recv()
        mixed = mixed + share_of(plane, yzr[j])
    done = mixed.astype(BF16)
    fin[0] = done
    last = send(fin.at[0], fin.at[1], f_s, f_r, u, ox)
    out[:, half_of(x)] = done
    last.wait_recv()
    out[:, half_of(ox)] = fin[1]
    for copy in pending:
        copy.wait_send()


def layer(query, new_key, new_value, lengths, residual, gain, router_t, ids, ids_t, key_cache, value_cache, out_w, gate_w, up_w, down_w):
    rows = residual.shape[0]
    block = residual.shape[1]
    half = block // CUTS
    cap = rows * 5 // 8
    hidden_units = gate_w.shape[1]
    count = PLANES * CORES * CUTS
    vmem = pl.BlockSpec(memory_space=pltpu.VMEM)
    hbm = pl.BlockSpec(memory_space=pl.ANY)
    dma = pltpu.SemaphoreType.DMA
    return pl.pallas_call(
        layer_kernel,
        out_shape=jax.ShapeDtypeStruct((rows, block), BF16),
        in_specs=[vmem] * 3 + [pl.BlockSpec(memory_space=pltpu.SMEM)] + [vmem] * 5 + [hbm] * 6,
        out_specs=vmem,
        scratch_shapes=[
            pltpu.VMEM(out_w.shape, BF16),
            pltpu.VMEM((W_SLOTS, block, hidden_units), BF16),
            pltpu.VMEM((W_SLOTS, block, hidden_units), BF16),
            pltpu.VMEM((D_SLOTS, hidden_units, block), BF16),
            pltpu.VMEM((query.shape[0], query.shape[1] // HD, HD), F32),
            pltpu.VMEM((query.shape[0], query.shape[1] // HD, HD), F32),
            pltpu.VMEM(new_key.shape, F32),
            pltpu.VMEM(new_value.shape, F32),
            pltpu.VMEM((rows, query.shape[1]), BF16),
            pltpu.VMEM((rows, half), BF16),
            pltpu.VMEM((rows, half), BF16),
            pltpu.VMEM((rows, half), F32),
            pltpu.VMEM((PLANES, cap, half), BF16),
            pltpu.VMEM((cap, D), BF16),
            pltpu.VMEM((cap, hidden_units), F32),
            pltpu.VMEM((cap, hidden_units), F32),
            pltpu.VMEM((cap, hidden_units), BF16),
            pltpu.VMEM((cap, block), F32),
            pltpu.VMEM((PLANES, cap, block), BF16),
            pltpu.VMEM((PLANES, cap, block), BF16),
            pltpu.VMEM((PLANES, cap, half), BF16),
            pltpu.VMEM((PLANES, cap, half), BF16),
            pltpu.VMEM((PLANES, cap, half), BF16),
            pltpu.VMEM((PLANES, cap, half), BF16),
            pltpu.VMEM((2, rows, half), BF16),
            pltpu.VMEM((8, rows), F32),
            pltpu.VMEM((count, 8, rows), F32),
            dma(()), dma((W_SLOTS,)), dma((W_SLOTS,)), dma((D_SLOTS,)), dma((D_SLOTS, 4)),
            dma((4,)), dma((4,)), dma((4,)), dma((4,)), dma(()), dma(()),
            dma((4,)), dma((4,)), dma((4,)), dma((4,)), dma((8,)), dma((8,)),
            dma((count,)), dma((count,)),
            dma((4,)), dma((4,)), dma((4,)), dma((4,)), dma((4,)), dma((4,)),
            dma(()), dma(()),
        ],
        compiler_params=pltpu.CompilerParams(
            collective_id=0, has_side_effects=True, vmem_limit_bytes=VMEM_MIB * 2**20
        ),
        name="layer",
    )(query, new_key, new_value, lengths, residual, gain, router_t, ids, ids_t, key_cache, value_cache, out_w, gate_w, up_w, down_w)


VMEM_MIB = 62


def fused_shards(
    residual, query, key_cache, value_cache, new_key, new_value, lengths, out_weight,
    router_weight, norm_gain, expert_ids, gate_weight, up_weight, down_weight,
):
    router_t = jnp.pad(router_weight.T, ((0, 8 - EXPERTS), (0, 0)))
    return layer(
        query, new_key, new_value, lengths, residual, norm_gain[None, :], router_t, expert_ids, expert_ids.T,
        key_cache, value_cache, out_weight, gate_weight, up_weight, down_weight,
    )


def solution(mesh):
    placed = (
        P("groups", "units"),
        P(("groups", "units"), "cuts"),
        P(("groups", "units"), None, "cuts"),
        P(("groups", "units"), None, "cuts"),
        P(("groups", "units"), "cuts"),
        P(("groups", "units"), "cuts"),
        P(("groups", "units")),
        P("cuts", "units"),
        P("units", None),
        P("units"),
        P("groups", None),
        P(None, ("units", "cuts")),
        P(None, ("units", "cuts")),
        P(("units", "cuts"), None),
    )
    fits = (mesh.shape["units"], mesh.shape["cuts"]) == (PLANES * CORES, CUTS)
    return jax.shard_map(
        fused_shards if fits else shards, mesh=mesh, in_specs=placed, out_specs=P("groups", "units"), check_vma=False
    )
```

```python
import functools

import jax
import jax.numpy as jnp
from jax import lax
from jax.experimental import pallas as pl
from jax.experimental.pallas import tpu as pltpu
from jax.sharding import PartitionSpec as P

D = 6144
HD = 128
EXPERTS = 4


eps = 1e-05


def attend(query, key_cache, value_cache, new_key, new_value, lengths):
    row_count = query.shape[0]
    slot_count = key_cache.shape[1]
    kv_local = key_cache.shape[2] // HD
    share = query.shape[1] // HD // kv_local
    scale_factor = HD ** (-0.5)
    q_heads = query.reshape(row_count, kv_local, share, HD)
    keys_all = key_cache.reshape(row_count, slot_count, kv_local, HD)
    values_all = value_cache.reshape(row_count, slot_count, kv_local, HD)
    key_own = new_key.reshape(row_count, kv_local, HD)
    value_own = new_value.reshape(row_count, kv_local, HD)
    scores = (
        jnp.einsum("rkgd,rtkd->rkgt", q_heads, keys_all, preferred_element_type=jnp.float32)
        * scale_factor
    )
    valid = (jnp.arange(slot_count, dtype=jnp.int32)[None, :] < lengths[:, None])[:, None, None, :]
    scores = jnp.where(valid, scores, -jnp.inf)
    own_score = (
        jnp.einsum("rkgd,rkd->rkg", q_heads, key_own, preferred_element_type=jnp.float32)
        * scale_factor
    )
    highest = jnp.maximum(jnp.max(scores, axis=-1), own_score)
    weights = jnp.exp(scores - highest[..., None])
    own_weight = jnp.exp(own_score - highest)
    total = jnp.sum(weights, axis=-1) + own_weight
    probs = (weights / total[..., None]).astype(jnp.bfloat16)
    own_prob = (own_weight / total).astype(jnp.bfloat16)
    heads_out = jnp.einsum("rkgt,rtkd->rkgd", probs, values_all, preferred_element_type=jnp.float32)
    heads_out = (
        heads_out
        + own_prob.astype(jnp.float32)[..., None] * value_own.astype(jnp.float32)[:, :, None, :]
    )
    return heads_out.reshape(row_count, kv_local * share * HD).astype(jnp.bfloat16)


def expert_block(rows_in, gate_weight, up_weight, down_weight):
    gate_part = jnp.dot(rows_in, gate_weight, preferred_element_type=jnp.float32)
    up_part = jnp.dot(rows_in, up_weight, preferred_element_type=jnp.float32)
    inner = (jax.nn.silu(gate_part) * up_part).astype(jnp.bfloat16)
    return jnp.dot(inner, down_weight, preferred_element_type=jnp.float32)


def shards(
    residual,
    query,
    key_cache,
    value_cache,
    new_key,
    new_value,
    lengths,
    out_weight,
    router_weight,
    norm_gain,
    expert_ids,
    gate_weight,
    up_weight,
    down_weight,
):
    attended = attend(query, key_cache, value_cache, new_key, new_value, lengths)
    partial_out = jnp.dot(
        lax.all_gather(attended, "units", axis=0, tiled=True),
        out_weight,
        preferred_element_type=jnp.float32,
    )
    projected = lax.psum(partial_out, "cuts")
    hidden_state = residual.astype(jnp.float32) + projected
    scaled = hidden_state * norm_gain
    local_squares = jnp.sum(hidden_state * hidden_state, axis=1)
    local_logits = jnp.dot(scaled, router_weight, precision=lax.Precision.HIGHEST)
    squares, logits_raw = lax.psum((local_squares, local_logits), "units")
    inv_rms = lax.rsqrt(squares / D + eps)
    logits = logits_raw * inv_rms[:, None]
    normed = (scaled * inv_rms[:, None]).astype(jnp.bfloat16)
    expert_range = jnp.arange(EXPERTS, dtype=jnp.int32)
    picked = (expert_ids[:, :, None] == expert_range[None, None, :]).astype(jnp.float32)
    chosen = jnp.sum(logits[:, None, :] * picked, axis=-1)
    gates = jax.nn.softmax(chosen, axis=1)
    per_expert = lax.axis_size("units") // EXPERTS
    expert_here = lax.axis_index("units") // per_expert
    weight_row = jnp.sum(gates * (expert_ids == expert_here).astype(jnp.float32), axis=1)
    rows_in = lax.all_gather(normed, "units", axis=1, tiled=True)
    expert_out = expert_block(rows_in, gate_weight, up_weight, down_weight)
    contribution = weight_row[:, None] * expert_out
    spread = lax.psum_scatter(
        contribution.astype(jnp.bfloat16), "units", scatter_dimension=1, tiled=True
    )
    mixture = lax.psum(spread, "cuts").astype(jnp.float32)
    return (hidden_state + mixture).astype(jnp.bfloat16)


F32 = jnp.float32
BF16 = jnp.bfloat16
W_SLOTS = 6
D_SLOTS = 4
PLANES = 4
CORES = 2
CUTS = 2


def partner(z, j):
    if j == 0:
        return z
    if j == 1:
        return z + 1 - 2 * lax.rem(z, 2)
    if j == 2:
        return lax.rem(z + 2, 4)
    return 3 - z


def dot(a, b, dims=((1,), (0,)), precision=None):
    return lax.dot_general(a, b, (dims, ((), ())), precision=precision, preferred_element_type=F32)


def layer_kernel(
    query, new_key, new_value, lengths, residual, gain, router_t, ids_t, key_cache, value_cache, out_w, gate_w, up_w, down_w,
    out,
    wo, wg, wu, wd, qs, os, nk, nv, a, psend, precv, hid, xs, x_in, accg, accu, inner,
    ycs, ycr, yxs, yxr, yzs, yzr, fin, ssend, srecv,
    sem_o, sem_g, sem_u, sem_d, sem_kv,
    gz_s, gz_r, gc_s, gc_r, p_s, p_r, dz_s, dz_r, dx_s, dx_r, dc_s, dc_r,
    st_s, st_r, yc_s, yc_r, yx_s, yx_r, yz_s, yz_r, f_s, f_r,
):
    g, u, x = lax.axis_index("groups"), lax.axis_index("units"), lax.axis_index("cuts")
    z, c = u // CORES, lax.rem(u, CORES)
    rows = a.shape[0]
    row_block = query.shape[0]
    block = wd.shape[2]
    half = block // CUTS
    cap = x_in.shape[0]
    units = PLANES * CORES
    count = units * CUTS
    me = u * CUTS + x
    ox, oc = 1 - x, 1 - c
    pending = []

    def unit(plane, core):
        return plane * CORES + core

    def remote(src, dst, ss, rs, to_unit, to_cut):
        return pltpu.make_async_remote_copy(
            src_ref=src, dst_ref=dst, send_sem=ss, recv_sem=rs,
            device_id=(g, to_unit, to_cut), device_id_type=pl.DeviceIdType.MESH,
        )

    def send(*args):
        copy = remote(*args)
        copy.start()
        pending.append(copy)
        return copy

    slots = key_cache.shape[1]
    lanes = key_cache.shape[2] // 2
    per_step = wd.shape[1] // slots
    steps = row_block // per_step

    def cache_copies(part, step, slot):
        for i in range(per_step):
            for n, cache in enumerate((key_cache, value_cache)):
                yield pltpu.make_async_copy(
                    cache.at[per_step * step + i, :, pl.ds(part * lanes, lanes)],
                    wd.at[slot, pl.ds(i * slots, slots), pl.ds(n * lanes, lanes)],
                    sem_kv.at[slot, 2 * i + n],
                )

    for step in range(steps):
        for copy in cache_copies(0, step, step):
            copy.start()
    copy_o = pltpu.make_async_copy(out_w, wo, sem_o)
    copy_o.start()

    barrier = pltpu.get_barrier_semaphore()
    for k in range(1, count):
        t = lax.rem(me + k, count)
        pl.semaphore_signal(barrier, inc=1, device_id=(g, t // CUTS, lax.rem(t, CUTS)), device_id_type=pl.DeviceIdType.MESH)

    def cols_of(index):
        return pl.ds(pl.multiple_of(index * block, 128), block)

    chunks = [(j, own) for j in range(PLANES) for own in (True, False)]

    def chunk_unit(k):
        j, own = chunks[k]
        return unit(partner(z, j), c if own else oc)

    def weight_copies(k):
        slot = k % W_SLOTS
        part = pl.ds(pl.multiple_of(chunk_unit(k) * block, 128), block)
        return (
            pltpu.make_async_copy(gate_w.at[part, :], wg.at[slot], sem_g.at[slot]),
            pltpu.make_async_copy(up_w.at[part, :], wu.at[slot], sem_u.at[slot]),
        )

    def start_weights(k):
        for copy in weight_copies(k):
            copy.start()

    d_chunks = [(j, own) for j in (3, 2, 1, 0) for own in (False, True)]

    def down_copy(k):
        j, own = d_chunks[k]
        slot = k % D_SLOTS
        return pltpu.make_async_copy(down_w.at[:, cols_of(unit(partner(z, j), c if own else oc))], wd.at[slot], sem_d.at[slot])

    def rows_of(index):
        return pl.ds(pl.multiple_of(index * row_block, 16), row_block)

    heads = query.shape[1] // HD // 2
    kv_heads = lanes // HD
    share = heads // kv_heads
    width = heads * HD
    qs[...] = query[...].astype(F32).reshape(row_block, 2 * heads, HD)
    own_head = (
        lax.broadcasted_iota(jnp.int32, (heads, lanes), 0) // share
        == lax.broadcasted_iota(jnp.int32, (heads, lanes), 1) // HD
    )
    slot_iota = lax.broadcasted_iota(jnp.int32, (heads, slots), 1)
    nk[...] = new_key[...].astype(F32)
    nv[...] = new_value[...].astype(F32)

    def attend_step(part, step):
        for copy in cache_copies(part, step, step):
            copy.wait()
        for i in range(per_step):
            row = per_step * step + i
            here = slice(part * lanes, (part + 1) * lanes)
            q = qs[row, part * heads:(part + 1) * heads, :]
            q = jnp.where(own_head, jnp.concatenate([q] * kv_heads, axis=1), 0.0)
            keys = wd[step, pl.ds(i * slots, slots), pl.ds(0, lanes)]
            values = wd[step, pl.ds(i * slots, slots), pl.ds(lanes, lanes)]
            scores = dot(q.astype(BF16), keys, ((1,), (1,))) * HD ** (-0.5)
            own = jnp.sum(q * nk[pl.ds(row, 1), here], axis=1, keepdims=True) * HD ** (-0.5)
            valid = slot_iota < lengths[row]
            highest = jnp.maximum(jnp.max(jnp.where(valid, scores, -jnp.inf), axis=1, keepdims=True), own)
            weights = jnp.where(valid, jnp.exp(jnp.where(valid, scores - highest, 0.0)), 0.0)
            own_weight = jnp.exp(own - highest)
            all_weight = jnp.sum(weights, axis=1, keepdims=True) + own_weight
            probs = (weights / all_weight).astype(BF16)
            own_prob = (own_weight / all_weight).astype(BF16).astype(F32)
            mix = dot(probs, values) + own_prob * nv[pl.ds(row, 1), here]
            mix = jnp.where(own_head, mix, 0.0)
            heads_out = mix[:, :HD]
            for n in range(1, kv_heads):
                heads_out = heads_out + mix[:, n * HD:(n + 1) * HD]
            os[part, row] = heads_out

    def part_of(index, part):
        return a.at[rows_of(index), pl.ds(part * width, width)]

    def spread_rows(part):
        a[rows_of(u), pl.ds(part * width, width)] = os[part].reshape(row_block, width).astype(BF16)
        if part == 0:
            pl.semaphore_wait(barrier, count - 1)
        mine = part_of(u, part)
        for j in (3, 2, 1):
            send(mine, mine, gz_s.at[4 * part + j], gz_r.at[4 * part + j], unit(partner(z, j), c), x)
        send(mine, mine, gc_s.at[4 * part], gc_r.at[4 * part], unit(z, oc), x)

    def gather_rows(part):
        for j in (3, 2, 1):
            there = unit(partner(z, j), c)
            got = part_of(there, part)
            remote(got, got, gz_s.at[4 * part + j], gz_r.at[4 * part + j], there, x).wait_recv()
            send(got, got, gc_s.at[4 * part + j], gc_r.at[4 * part + j], unit(z, oc), x)
        for j in range(PLANES):
            got = part_of(unit(partner(z, j), oc), part)
            remote(got, got, gc_s.at[4 * part + j], gc_r.at[4 * part + j], unit(z, oc), x).wait_recv()

    @pl.loop(0, steps)
    def _(step):
        attend_step(0, step)
        for copy in cache_copies(1, step, step):
            copy.start()

    for k in range(W_SLOTS):
        start_weights(k)
    spread_rows(0)

    @pl.loop(0, steps)
    def _(step):
        attend_step(1, step)

    spread_rows(1)
    for k in range(D_SLOTS):
        down_copy(k).start()
    copy_o.wait()

    ids_row = ids_t[...]
    e_iota = lax.broadcasted_iota(jnp.int32, (8, rows), 0)
    named_t = (ids_row[0:1, :] == e_iota) | (ids_row[1:2, :] == e_iota)
    r0 = lax.broadcasted_iota(jnp.int32, (rows, rows), 0)
    r1 = lax.broadcasted_iota(jnp.int32, (rows, rows), 1)
    upper = jnp.where(r0 <= r1, 1.0, 0.0)
    place_t = dot(jnp.where(named_t, 1.0, 0.0), upper)
    place_t = jnp.where(named_t, place_t, 0.0)
    s_iota = (lax.broadcasted_iota(jnp.int32, (cap, rows), 0) + 1).astype(F32)

    def pick(row):
        return jnp.where(row == s_iota, 1.0, 0.0)

    def half_of(index):
        return pl.ds(pl.multiple_of(index * half, 128), half)

    def project(part, cut):
        here = pl.ds(part * width, width)
        return dot(a[:, here], wo[here, half_of(cut)])

    gather_rows(0)
    other_part = project(0, ox)
    hid[...] = project(0, x) + residual[:, half_of(x)].astype(F32)
    gather_rows(1)
    psend[...] = (other_part + project(1, ox)).astype(BF16)
    psum_copy = send(psend, precv, p_s, p_r, u, ox)
    own_part = hid[...] + project(1, x)
    psum_copy.wait_recv()
    hidden = own_part + precv[...].astype(F32)
    hid[...] = hidden
    all_gain = gain[...].reshape(1, block)
    scaled = hidden * jnp.where(x == 0, all_gain[:, :half], all_gain[:, half:])
    scaled16 = scaled.astype(BF16)

    def line_cols(plane, core, cut):
        return pl.ds(pl.multiple_of(unit(plane, core) * block + cut * half, 128), half)

    def place_row(expert):
        return jnp.sum(jnp.where(e_iota == expert, place_t, 0.0), axis=0, keepdims=True)

    for j in (1, 2, 3):
        to = partner(z, j)
        xs[j] = dot(pick(place_row(to)).astype(BF16), scaled16).astype(BF16)
        send(xs.at[j], x_in.at[:, line_cols(z, c, x)], dz_s.at[j], dz_r.at[j], unit(to, c), x)
    my_pick = pick(place_row(z))
    x_in[:, line_cols(z, c, x)] = dot(my_pick.astype(BF16), scaled16).astype(BF16)

    def spread(j):
        plane = partner(z, j)
        got = x_in.at[:, line_cols(plane, c, x)]
        if j:
            remote(got, got, dz_s.at[j], dz_r.at[j], unit(plane, c), x).wait_recv()
        send(got, got, dx_s.at[j], dx_r.at[j], u, ox)
        send(got, got, dc_s.at[2 * j], dc_r.at[2 * j], unit(z, oc), x)

    def relay(j):
        got = x_in.at[:, line_cols(partner(z, j), c, ox)]
        remote(got, got, dx_s.at[j], dx_r.at[j], u, ox).wait_recv()
        send(got, got, dc_s.at[2 * j + 1], dc_r.at[2 * j + 1], unit(z, oc), x)

    spread(0)
    high = lax.Precision.HIGHEST
    sq = dot(jnp.ones((8, half), F32), hidden * hidden, ((1,), (1,)), high)
    lg = dot(router_t[:, half_of(x)], scaled, ((1,), (1,)), high)
    stat = jnp.concatenate([lg, sq[EXPERTS:]], axis=0)
    ssend[...] = stat
    for k in range(1, count):
        t = lax.rem(me + k, count)
        send(ssend, srecv.at[me], st_s.at[k], st_r.at[me], t // CUTS, lax.rem(t, CUTS))

    def feed(k):
        j, own = chunks[k]
        if not own:
            for i in (0, 1):
                got = x_in.at[:, line_cols(partner(z, j), oc, x if i == 0 else ox)]
                remote(got, got, dc_s.at[2 * j + i], dc_r.at[2 * j + i], unit(z, oc), x).wait_recv()
        for copy in weight_copies(k):
            copy.wait()
        slot = k % W_SLOTS
        tile = 512

        @pl.loop(0, wg.shape[2] // tile)
        def _(i):
            cols = pl.ds(pl.multiple_of(i * tile, 128), tile)
            rows_x = x_in[:, cols_of(chunk_unit(k))]
            part_g = dot(rows_x, wg[slot, :, cols])
            part_u = dot(rows_x, wu[slot, :, cols])
            if k == 0:
                accg[:, cols] = part_g
                accu[:, cols] = part_u
            else:
                accg[:, cols] += part_g
                accu[:, cols] += part_u

        if k + W_SLOTS < len(chunks):
            start_weights(k + W_SLOTS)

    spread(1)
    relay(0)
    feed(0)
    spread(2)
    relay(1)
    feed(1)
    spread(3)
    relay(2)
    feed(2)
    relay(3)
    for k in range(3, len(chunks)):
        feed(k)

    total = stat
    for k in range(1, count):
        t = lax.rem(me + k, count)
        remote(ssend, srecv.at[t], st_s.at[k], st_r.at[t], t // CUTS, lax.rem(t, CUTS)).wait_recv()
        total = total + srecv[t]
    inv = lax.rsqrt(jnp.sum(jnp.where(e_iota == 4, total, 0.0), axis=0, keepdims=True) / D + eps)
    inv_col = jnp.sum(my_pick * inv, axis=1, keepdims=True)
    tile = 512

    @pl.loop(0, inner.shape[1] // tile)
    def _(i):
        cols = pl.ds(pl.multiple_of(i * tile, 128), tile)
        gate_part = accg[:, cols] * inv_col
        up_part = accu[:, cols] * inv_col
        inner[:, cols] = (gate_part * jax.nn.sigmoid(gate_part) * up_part).astype(BF16)

    def down_part(k, dst):
        down_copy(k).wait()
        slot = k % D_SLOTS
        tile = 256

        @pl.loop(0, block // tile)
        def _(i):
            cols = pl.ds(pl.multiple_of(i * tile, 128), tile)
            dst[:, cols] = dot(inner[...], wd[slot, :, cols]).astype(dst.dtype)

        if k + D_SLOTS < len(d_chunks):
            down_copy(k + D_SLOTS).start()

    order = (3, 2, 1, 0)
    yf = [acc.at[:, pl.ds(0, block)] for acc in (accg, accu)]

    def core_stage(n):
        j = order[n]
        remote(ycs.at[j], ycr.at[j], yc_s.at[j], yc_r.at[j], unit(z, oc), x).wait_recv()
        yxs[j] = (yf[n % 2][:, half_of(ox)] + ycr[j, :, half_of(ox)].astype(F32)).astype(BF16)
        send(yxs.at[j], yxr.at[j], yx_s.at[j], yx_r.at[j], u, ox)

    def cut_stage(n):
        j = order[n]
        mine = yf[n % 2][:, half_of(x)] + ycr[j, :, half_of(x)].astype(F32)
        remote(yxs.at[j], yxr.at[j], yx_s.at[j], yx_r.at[j], u, ox).wait_recv()
        yzs[j] = (mine + yxr[j].astype(F32)).astype(BF16)
        if j:
            send(yzs.at[j], yzr.at[j], yz_s.at[j], yz_r.at[j], unit(partner(z, j), c), x)

    for n, j in enumerate(order):
        down_part(2 * n, ycs.at[j])
        send(ycs.at[j], ycr.at[j], yc_s.at[j], yc_r.at[j], unit(z, oc), x)
        if n:
            core_stage(n - 1)
        down_part(2 * n + 1, yf[n % 2])
        if n:
            cut_stage(n - 1)
    core_stage(len(order) - 1)

    logits = total * inv
    top = jnp.max(jnp.where(named_t, logits, -jnp.inf), axis=0, keepdims=True)
    raised = jnp.where(named_t, jnp.exp(jnp.where(named_t, logits - top, 0.0)), 0.0)
    gates = raised / jnp.sum(raised, axis=0, keepdims=True)
    spot = (lax.broadcasted_iota(jnp.int32, (rows, cap), 1) + 1).astype(F32)

    def share_of(expert, contribution):
        weight = jnp.sum(jnp.where(r0 == r1, jnp.sum(jnp.where(e_iota == expert, gates, 0.0), axis=0, keepdims=True), 0.0), axis=1, keepdims=True)
        column = jnp.sum(jnp.where(r0 == r1, place_row(expert), 0.0), axis=1, keepdims=True)
        return weight * dot(jnp.where(column == spot, 1.0, 0.0).astype(BF16), contribution)

    mixed = hid[...]
    for j in (3, 2, 1):
        plane = partner(z, j)
        remote(yzs.at[j], yzr.at[j], yz_s.at[j], yz_r.at[j], unit(plane, c), x).wait_recv()
        mixed = mixed + share_of(plane, yzr[j])
    cut_stage(len(order) - 1)
    mixed = mixed + share_of(z, yzs[0])
    done = mixed.astype(BF16)
    fin[0] = done
    last = send(fin.at[0], fin.at[1], f_s, f_r, u, ox)
    out[:, half_of(x)] = done
    last.wait_recv()
    out[:, half_of(ox)] = fin[1]
    for copy in pending:
        copy.wait_send()


def layer(query, new_key, new_value, lengths, residual, gain, router_t, ids_t, key_cache, value_cache, out_w, gate_w, up_w, down_w):
    rows = residual.shape[0]
    block = residual.shape[1]
    half = block // CUTS
    cap = rows * 5 // 8
    hidden_units = gate_w.shape[1]
    count = PLANES * CORES * CUTS
    vmem = pl.BlockSpec(memory_space=pltpu.VMEM)
    hbm = pl.BlockSpec(memory_space=pl.ANY)
    dma = pltpu.SemaphoreType.DMA
    return pl.pallas_call(
        layer_kernel,
        out_shape=jax.ShapeDtypeStruct((rows, block), BF16),
        in_specs=[vmem] * 3 + [pl.BlockSpec(memory_space=pltpu.SMEM)] + [vmem] * 4 + [hbm] * 6,
        out_specs=vmem,
        scratch_shapes=[
            pltpu.VMEM(out_w.shape, BF16),
            pltpu.VMEM((W_SLOTS, block, hidden_units), BF16),
            pltpu.VMEM((W_SLOTS, block, hidden_units), BF16),
            pltpu.VMEM((D_SLOTS, hidden_units, block), BF16),
            pltpu.VMEM((query.shape[0], query.shape[1] // HD, HD), F32),
            pltpu.VMEM((2, query.shape[0], query.shape[1] // HD // 2, HD), F32),
            pltpu.VMEM(new_key.shape, F32),
            pltpu.VMEM(new_value.shape, F32),
            pltpu.VMEM((rows, query.shape[1]), BF16),
            pltpu.VMEM((rows, half), BF16),
            pltpu.VMEM((rows, half), BF16),
            pltpu.VMEM((rows, half), F32),
            pltpu.VMEM((PLANES, cap, half), BF16),
            pltpu.VMEM((cap, D), BF16),
            pltpu.VMEM((cap, hidden_units), F32),
            pltpu.VMEM((cap, hidden_units), F32),
            pltpu.VMEM((cap, hidden_units), BF16),
            pltpu.VMEM((PLANES, cap, block), BF16),
            pltpu.VMEM((PLANES, cap, block), BF16),
            pltpu.VMEM((PLANES, cap, half), BF16),
            pltpu.VMEM((PLANES, cap, half), BF16),
            pltpu.VMEM((PLANES, cap, half), BF16),
            pltpu.VMEM((PLANES, cap, half), BF16),
            pltpu.VMEM((2, rows, half), BF16),
            pltpu.VMEM((8, rows), F32),
            pltpu.VMEM((count, 8, rows), F32),
            dma(()), dma((W_SLOTS,)), dma((W_SLOTS,)), dma((D_SLOTS,)), dma((D_SLOTS, 8)),
            dma((8,)), dma((8,)), dma((8,)), dma((8,)), dma(()), dma(()),
            dma((4,)), dma((4,)), dma((4,)), dma((4,)), dma((8,)), dma((8,)),
            dma((count,)), dma((count,)),
            dma((4,)), dma((4,)), dma((4,)), dma((4,)), dma((4,)), dma((4,)),
            dma(()), dma(()),
        ],
        compiler_params=pltpu.CompilerParams(
            collective_id=0, has_side_effects=True, vmem_limit_bytes=VMEM_MIB * 2**20
        ),
        name="layer",
    )(query, new_key, new_value, lengths, residual, gain, router_t, ids_t, key_cache, value_cache, out_w, gate_w, up_w, down_w)


VMEM_MIB = 62


def fused_shards(
    residual, query, key_cache, value_cache, new_key, new_value, lengths, out_weight,
    router_weight, norm_gain, expert_ids, gate_weight, up_weight, down_weight,
):
    return layer(
        query, new_key, new_value, lengths, residual, norm_gain, router_weight.T, expert_ids.T,
        key_cache, value_cache, out_weight, gate_weight, up_weight, down_weight,
    )


def solution(mesh):
    placed = (
        P("groups", "units"),
        P(("groups", "units"), "cuts"),
        P(("groups", "units"), None, "cuts"),
        P(("groups", "units"), None, "cuts"),
        P(("groups", "units"), "cuts"),
        P(("groups", "units"), "cuts"),
        P(("groups", "units")),
        P("cuts", "units"),
        P("units", None),
        P("units"),
        P("groups", None),
        P(None, ("units", "cuts")),
        P(None, ("units", "cuts")),
        P(("units", "cuts"), None),
    )
    fits = (mesh.shape["units"], mesh.shape["cuts"]) == (PLANES * CORES, CUTS)
    return jax.shard_map(
        fused_shards if fits else shards, mesh=mesh, in_specs=placed, out_specs=P("groups", "units"), check_vma=False
    )
```

```python
import functools

import jax
import jax.numpy as jnp
from jax import lax
from jax.experimental import pallas as pl
from jax.experimental.pallas import tpu as pltpu
from jax.sharding import PartitionSpec as P

D = 6144
HD = 128
EXPERTS = 4


eps = 1e-05


def attend(query, key_cache, value_cache, new_key, new_value, lengths):
    row_count = query.shape[0]
    slot_count = key_cache.shape[1]
    kv_local = key_cache.shape[2] // HD
    share = query.shape[1] // HD // kv_local
    scale_factor = HD ** (-0.5)
    q_heads = query.reshape(row_count, kv_local, share, HD)
    keys_all = key_cache.reshape(row_count, slot_count, kv_local, HD)
    values_all = value_cache.reshape(row_count, slot_count, kv_local, HD)
    key_own = new_key.reshape(row_count, kv_local, HD)
    value_own = new_value.reshape(row_count, kv_local, HD)
    scores = (
        jnp.einsum("rkgd,rtkd->rkgt", q_heads, keys_all, preferred_element_type=jnp.float32)
        * scale_factor
    )
    valid = (jnp.arange(slot_count, dtype=jnp.int32)[None, :] < lengths[:, None])[:, None, None, :]
    scores = jnp.where(valid, scores, -jnp.inf)
    own_score = (
        jnp.einsum("rkgd,rkd->rkg", q_heads, key_own, preferred_element_type=jnp.float32)
        * scale_factor
    )
    highest = jnp.maximum(jnp.max(scores, axis=-1), own_score)
    weights = jnp.exp(scores - highest[..., None])
    own_weight = jnp.exp(own_score - highest)
    total = jnp.sum(weights, axis=-1) + own_weight
    probs = (weights / total[..., None]).astype(jnp.bfloat16)
    own_prob = (own_weight / total).astype(jnp.bfloat16)
    heads_out = jnp.einsum("rkgt,rtkd->rkgd", probs, values_all, preferred_element_type=jnp.float32)
    heads_out = (
        heads_out
        + own_prob.astype(jnp.float32)[..., None] * value_own.astype(jnp.float32)[:, :, None, :]
    )
    return heads_out.reshape(row_count, kv_local * share * HD).astype(jnp.bfloat16)


def expert_block(rows_in, gate_weight, up_weight, down_weight):
    gate_part = jnp.dot(rows_in, gate_weight, preferred_element_type=jnp.float32)
    up_part = jnp.dot(rows_in, up_weight, preferred_element_type=jnp.float32)
    inner = (jax.nn.silu(gate_part) * up_part).astype(jnp.bfloat16)
    return jnp.dot(inner, down_weight, preferred_element_type=jnp.float32)


def shards(
    residual,
    query,
    key_cache,
    value_cache,
    new_key,
    new_value,
    lengths,
    out_weight,
    router_weight,
    norm_gain,
    expert_ids,
    gate_weight,
    up_weight,
    down_weight,
):
    attended = attend(query, key_cache, value_cache, new_key, new_value, lengths)
    partial_out = jnp.dot(
        lax.all_gather(attended, "units", axis=0, tiled=True),
        out_weight,
        preferred_element_type=jnp.float32,
    )
    projected = lax.psum(partial_out, "cuts")
    hidden_state = residual.astype(jnp.float32) + projected
    scaled = hidden_state * norm_gain
    local_squares = jnp.sum(hidden_state * hidden_state, axis=1)
    local_logits = jnp.dot(scaled, router_weight, precision=lax.Precision.HIGHEST)
    squares, logits_raw = lax.psum((local_squares, local_logits), "units")
    inv_rms = lax.rsqrt(squares / D + eps)
    logits = logits_raw * inv_rms[:, None]
    normed = (scaled * inv_rms[:, None]).astype(jnp.bfloat16)
    expert_range = jnp.arange(EXPERTS, dtype=jnp.int32)
    picked = (expert_ids[:, :, None] == expert_range[None, None, :]).astype(jnp.float32)
    chosen = jnp.sum(logits[:, None, :] * picked, axis=-1)
    gates = jax.nn.softmax(chosen, axis=1)
    per_expert = lax.axis_size("units") // EXPERTS
    expert_here = lax.axis_index("units") // per_expert
    weight_row = jnp.sum(gates * (expert_ids == expert_here).astype(jnp.float32), axis=1)
    rows_in = lax.all_gather(normed, "units", axis=1, tiled=True)
    expert_out = expert_block(rows_in, gate_weight, up_weight, down_weight)
    contribution = weight_row[:, None] * expert_out
    spread = lax.psum_scatter(
        contribution.astype(jnp.bfloat16), "units", scatter_dimension=1, tiled=True
    )
    mixture = lax.psum(spread, "cuts").astype(jnp.float32)
    return (hidden_state + mixture).astype(jnp.bfloat16)


F32 = jnp.float32
BF16 = jnp.bfloat16
W_SLOTS = 6
D_SLOTS = 4
PLANES = 4
CORES = 2
CUTS = 2


def partner(z, j):
    if j == 0:
        return z
    if j == 1:
        return z + 1 - 2 * lax.rem(z, 2)
    if j == 2:
        return lax.rem(z + 2, 4)
    return 3 - z


def dot(a, b, dims=((1,), (0,)), precision=None):
    return lax.dot_general(a, b, (dims, ((), ())), precision=precision, preferred_element_type=F32)


def layer_kernel(
    query, new_key, new_value, lengths, residual, gain, router_t, ids_t, key_cache, value_cache, out_w, gate_w, up_w, down_w,
    out,
    wo, wg, wu, wd, qs, os, nk, nv, a, psend, precv, hid, xs, x_in, accg, accu, inner,
    ycs, ycr, yxs, yxr, yzs, yzr, fin, ssend, srecv,
    sem_o, sem_g, sem_u, sem_d, sem_kv,
    gz_s, gz_r, gc_s, gc_r, p_s, p_r, dz_s, dz_r, dx_s, dx_r, dc_s, dc_r,
    st_s, st_r, yc_s, yc_r, yx_s, yx_r, yz_s, yz_r, f_s, f_r,
):
    g, u, x = lax.axis_index("groups"), lax.axis_index("units"), lax.axis_index("cuts")
    z, c = u // CORES, lax.rem(u, CORES)
    rows = a.shape[0]
    row_block = query.shape[0]
    block = wd.shape[2]
    half = block // CUTS
    cap = x_in.shape[0]
    units = PLANES * CORES
    count = units * CUTS
    me = u * CUTS + x
    ox, oc = 1 - x, 1 - c
    pending = []

    def unit(plane, core):
        return plane * CORES + core

    def remote(src, dst, ss, rs, to_unit, to_cut):
        return pltpu.make_async_remote_copy(
            src_ref=src, dst_ref=dst, send_sem=ss, recv_sem=rs,
            device_id=(g, to_unit, to_cut), device_id_type=pl.DeviceIdType.MESH,
        )

    def send(*args):
        copy = remote(*args)
        copy.start()
        pending.append(copy)
        return copy

    slots = key_cache.shape[1]
    lanes = key_cache.shape[2] // 2
    per_step = wd.shape[1] // slots
    steps = row_block // per_step

    def cache_copies(part, step, slot):
        for i in range(per_step):
            for n, cache in enumerate((key_cache, value_cache)):
                yield pltpu.make_async_copy(
                    cache.at[per_step * step + i, :, pl.ds(part * lanes, lanes)],
                    wd.at[slot, pl.ds(i * slots, slots), pl.ds(n * lanes, lanes)],
                    sem_kv.at[slot, 2 * i + n],
                )

    for step in range(steps):
        for copy in cache_copies(0, step, step):
            copy.start()
    copy_o = pltpu.make_async_copy(out_w, wo, sem_o)
    copy_o.start()

    barrier = pltpu.get_barrier_semaphore()
    for k in range(1, count):
        t = lax.rem(me + k, count)
        pl.semaphore_signal(barrier, inc=1, device_id=(g, t // CUTS, lax.rem(t, CUTS)), device_id_type=pl.DeviceIdType.MESH)

    def cols_of(index):
        return pl.ds(pl.multiple_of(index * block, 128), block)

    chunks = [(j, own) for j in range(PLANES) for own in (True, False)]

    def chunk_unit(k):
        j, own = chunks[k]
        return unit(partner(z, j), c if own else oc)

    def weight_copies(k):
        slot = k % W_SLOTS
        part = pl.ds(pl.multiple_of(chunk_unit(k) * block, 128), block)
        return (
            pltpu.make_async_copy(gate_w.at[part, :], wg.at[slot], sem_g.at[slot]),
            pltpu.make_async_copy(up_w.at[part, :], wu.at[slot], sem_u.at[slot]),
        )

    def start_weights(k):
        for copy in weight_copies(k):
            copy.start()

    d_chunks = [(j, own) for j in (3, 2, 1, 0) for own in (False, True)]

    def down_copy(k):
        j, own = d_chunks[k]
        slot = k % D_SLOTS
        return pltpu.make_async_copy(down_w.at[:, cols_of(unit(partner(z, j), c if own else oc))], wd.at[slot], sem_d.at[slot])

    def rows_of(index):
        return pl.ds(pl.multiple_of(index * row_block, 16), row_block)

    heads = query.shape[1] // HD // 2
    kv_heads = lanes // HD
    share = heads // kv_heads
    width = heads * HD
    qs[...] = query[...].astype(F32).reshape(row_block, 2 * heads, HD)
    own_head = (
        lax.broadcasted_iota(jnp.int32, (heads, lanes), 0) // share
        == lax.broadcasted_iota(jnp.int32, (heads, lanes), 1) // HD
    )
    slot_iota = lax.broadcasted_iota(jnp.int32, (heads, slots), 1)
    nk[...] = new_key[...].astype(F32)
    nv[...] = new_value[...].astype(F32)

    def attend_step(part, step):
        for copy in cache_copies(part, step, step):
            copy.wait()
        for i in range(per_step):
            row = per_step * step + i
            here = slice(part * lanes, (part + 1) * lanes)
            q = qs[row, part * heads:(part + 1) * heads, :]
            q = jnp.where(own_head, jnp.concatenate([q] * kv_heads, axis=1), 0.0)
            keys = wd[step, pl.ds(i * slots, slots), pl.ds(0, lanes)]
            values = wd[step, pl.ds(i * slots, slots), pl.ds(lanes, lanes)]
            scores = dot(q.astype(BF16), keys, ((1,), (1,))) * HD ** (-0.5)
            own = jnp.sum(q * nk[pl.ds(row, 1), here], axis=1, keepdims=True) * HD ** (-0.5)
            valid = slot_iota < lengths[row]
            scores = jnp.where(valid, scores, -jnp.inf)
            highest = jnp.maximum(jnp.max(scores, axis=1, keepdims=True), own)
            weights = jnp.exp(scores - highest)
            own_weight = jnp.exp(own - highest)
            all_weight = jnp.sum(weights, axis=1, keepdims=True) + own_weight
            probs = (weights * (1.0 / all_weight)).astype(BF16)
            own_prob = (own_weight / all_weight).astype(BF16).astype(F32)
            mix = dot(probs, values) + own_prob * nv[pl.ds(row, 1), here]
            mix = jnp.where(own_head, mix, 0.0)
            heads_out = mix[:, :HD]
            for n in range(1, kv_heads):
                heads_out = heads_out + mix[:, n * HD:(n + 1) * HD]
            os[part, row] = heads_out

    def part_of(index, part):
        return a.at[rows_of(index), pl.ds(part * width, width)]

    def spread_rows(part):
        a[rows_of(u), pl.ds(part * width, width)] = os[part].reshape(row_block, width).astype(BF16)
        if part == 0:
            pl.semaphore_wait(barrier, count - 1)
        mine = part_of(u, part)
        for j in (3, 2, 1):
            send(mine, mine, gz_s.at[4 * part + j], gz_r.at[4 * part + j], unit(partner(z, j), c), x)
        send(mine, mine, gc_s.at[4 * part], gc_r.at[4 * part], unit(z, oc), x)

    def gather_rows(part):
        for j in (3, 2, 1):
            there = unit(partner(z, j), c)
            got = part_of(there, part)
            remote(got, got, gz_s.at[4 * part + j], gz_r.at[4 * part + j], there, x).wait_recv()
            send(got, got, gc_s.at[4 * part + j], gc_r.at[4 * part + j], unit(z, oc), x)
        for j in range(PLANES):
            got = part_of(unit(partner(z, j), oc), part)
            remote(got, got, gc_s.at[4 * part + j], gc_r.at[4 * part + j], unit(z, oc), x).wait_recv()

    @pl.loop(0, steps)
    def _(step):
        attend_step(0, step)
        for copy in cache_copies(1, step, step):
            copy.start()

    for k in range(W_SLOTS):
        start_weights(k)
    spread_rows(0)

    @pl.loop(0, steps)
    def _(step):
        attend_step(1, step)

    spread_rows(1)
    for k in range(D_SLOTS):
        down_copy(k).start()
    copy_o.wait()

    ids_row = ids_t[...]
    e_iota = lax.broadcasted_iota(jnp.int32, (8, rows), 0)
    named_t = (ids_row[0:1, :] == e_iota) | (ids_row[1:2, :] == e_iota)
    r0 = lax.broadcasted_iota(jnp.int32, (rows, rows), 0)
    r1 = lax.broadcasted_iota(jnp.int32, (rows, rows), 1)
    upper = jnp.where(r0 <= r1, 1.0, 0.0)
    place_t = dot(jnp.where(named_t, 1.0, 0.0), upper)
    place_t = jnp.where(named_t, place_t, 0.0)
    s_iota = (lax.broadcasted_iota(jnp.int32, (cap, rows), 0) + 1).astype(F32)

    def pick(row):
        return jnp.where(row == s_iota, 1.0, 0.0)

    def half_of(index):
        return pl.ds(pl.multiple_of(index * half, 128), half)

    def project(part, cut):
        here = pl.ds(part * width, width)
        return dot(a[:, here], wo[here, half_of(cut)])

    gather_rows(0)
    other_part = project(0, ox)
    hid[...] = project(0, x) + residual[:, half_of(x)].astype(F32)
    gather_rows(1)
    psend[...] = (other_part + project(1, ox)).astype(BF16)
    psum_copy = send(psend, precv, p_s, p_r, u, ox)
    own_part = hid[...] + project(1, x)
    psum_copy.wait_recv()
    hidden = own_part + precv[...].astype(F32)
    hid[...] = hidden
    all_gain = gain[...].reshape(1, block)
    scaled = hidden * jnp.where(x == 0, all_gain[:, :half], all_gain[:, half:])
    scaled16 = scaled.astype(BF16)

    def line_cols(plane, core, cut):
        return pl.ds(pl.multiple_of(unit(plane, core) * block + cut * half, 128), half)

    def place_row(expert):
        return jnp.sum(jnp.where(e_iota == expert, place_t, 0.0), axis=0, keepdims=True)

    for j in (1, 2, 3):
        to = partner(z, j)
        xs[j] = dot(pick(place_row(to)).astype(BF16), scaled16).astype(BF16)
        send(xs.at[j], x_in.at[:, line_cols(z, c, x)], dz_s.at[j], dz_r.at[j], unit(to, c), x)
    my_pick = pick(place_row(z))
    x_in[:, line_cols(z, c, x)] = dot(my_pick.astype(BF16), scaled16).astype(BF16)

    def spread(j):
        plane = partner(z, j)
        got = x_in.at[:, line_cols(plane, c, x)]
        if j:
            remote(got, got, dz_s.at[j], dz_r.at[j], unit(plane, c), x).wait_recv()
        send(got, got, dx_s.at[j], dx_r.at[j], u, ox)
        send(got, got, dc_s.at[2 * j], dc_r.at[2 * j], unit(z, oc), x)

    def relay(j):
        got = x_in.at[:, line_cols(partner(z, j), c, ox)]
        remote(got, got, dx_s.at[j], dx_r.at[j], u, ox).wait_recv()
        send(got, got, dc_s.at[2 * j + 1], dc_r.at[2 * j + 1], unit(z, oc), x)

    spread(0)
    high = lax.Precision.HIGHEST
    sq = dot(jnp.ones((8, half), F32), hidden * hidden, ((1,), (1,)), high)
    lg = dot(router_t[:, half_of(x)], scaled, ((1,), (1,)), high)
    stat = jnp.concatenate([lg, sq[EXPERTS:]], axis=0)
    ssend[...] = stat
    for k in range(1, count):
        t = lax.rem(me + k, count)
        send(ssend, srecv.at[me], st_s.at[k], st_r.at[me], t // CUTS, lax.rem(t, CUTS))

    def feed(k):
        j, own = chunks[k]
        if not own:
            for i in (0, 1):
                got = x_in.at[:, line_cols(partner(z, j), oc, x if i == 0 else ox)]
                remote(got, got, dc_s.at[2 * j + i], dc_r.at[2 * j + i], unit(z, oc), x).wait_recv()
        for copy in weight_copies(k):
            copy.wait()
        slot = k % W_SLOTS
        tile = 512

        @pl.loop(0, wg.shape[2] // tile)
        def _(i):
            cols = pl.ds(pl.multiple_of(i * tile, 128), tile)
            rows_x = x_in[:, cols_of(chunk_unit(k))]
            part_g = dot(rows_x, wg[slot, :, cols])
            part_u = dot(rows_x, wu[slot, :, cols])
            if k == 0:
                accg[:, cols] = part_g
                accu[:, cols] = part_u
            else:
                accg[:, cols] += part_g
                accu[:, cols] += part_u

        if k + W_SLOTS < len(chunks):
            start_weights(k + W_SLOTS)

    spread(1)
    relay(0)
    feed(0)
    spread(2)
    relay(1)
    feed(1)
    spread(3)
    relay(2)
    feed(2)
    relay(3)
    for k in range(3, len(chunks)):
        feed(k)

    total = stat
    for k in range(1, count):
        t = lax.rem(me + k, count)
        remote(ssend, srecv.at[t], st_s.at[k], st_r.at[t], t // CUTS, lax.rem(t, CUTS)).wait_recv()
        total = total + srecv[t]
    inv = lax.rsqrt(jnp.sum(jnp.where(e_iota == 4, total, 0.0), axis=0, keepdims=True) / D + eps)
    inv_col = jnp.sum(my_pick * inv, axis=1, keepdims=True)
    tile = 512

    @pl.loop(0, inner.shape[1] // tile)
    def _(i):
        cols = pl.ds(pl.multiple_of(i * tile, 128), tile)
        gate_part = accg[:, cols] * inv_col
        up_part = accu[:, cols] * inv_col
        inner[:, cols] = (gate_part * jax.nn.sigmoid(gate_part) * up_part).astype(BF16)

    def down_part(k, dst):
        down_copy(k).wait()
        slot = k % D_SLOTS
        tile = 256

        @pl.loop(0, block // tile)
        def _(i):
            cols = pl.ds(pl.multiple_of(i * tile, 128), tile)
            dst[:, cols] = dot(inner[...], wd[slot, :, cols]).astype(dst.dtype)

        if k + D_SLOTS < len(d_chunks):
            down_copy(k + D_SLOTS).start()

    order = (3, 2, 1, 0)
    yf = [acc.at[:, pl.ds(n * block, block)] for acc in (accg, accu) for n in (0, 1)]

    def core_stage(n):
        j = order[n]
        remote(ycs.at[j], ycr.at[j], yc_s.at[j], yc_r.at[j], unit(z, oc), x).wait_recv()
        yxs[j] = (yf[n][:, half_of(ox)] + ycr[j, :, half_of(ox)].astype(F32)).astype(BF16)
        send(yxs.at[j], yxr.at[j], yx_s.at[j], yx_r.at[j], u, ox)

    def cut_stage(n):
        j = order[n]
        mine = yf[n][:, half_of(x)] + ycr[j, :, half_of(x)].astype(F32)
        remote(yxs.at[j], yxr.at[j], yx_s.at[j], yx_r.at[j], u, ox).wait_recv()
        yzs[j] = (mine + yxr[j].astype(F32)).astype(BF16)
        if j:
            send(yzs.at[j], yzr.at[j], yz_s.at[j], yz_r.at[j], unit(partner(z, j), c), x)

    for n, j in enumerate(order):
        down_part(2 * n, ycs.at[j])
        send(ycs.at[j], ycr.at[j], yc_s.at[j], yc_r.at[j], unit(z, oc), x)
        if n:
            core_stage(n - 1)
        down_part(2 * n + 1, yf[n])
        if n > 1:
            cut_stage(n - 2)
    core_stage(len(order) - 1)
    cut_stage(len(order) - 2)

    logits = total * inv
    top = jnp.max(jnp.where(named_t, logits, -jnp.inf), axis=0, keepdims=True)
    raised = jnp.where(named_t, jnp.exp(jnp.where(named_t, logits - top, 0.0)), 0.0)
    gates = raised / jnp.sum(raised, axis=0, keepdims=True)
    spot = (lax.broadcasted_iota(jnp.int32, (rows, cap), 1) + 1).astype(F32)

    def share_of(expert, contribution):
        weight = jnp.sum(jnp.where(r0 == r1, jnp.sum(jnp.where(e_iota == expert, gates, 0.0), axis=0, keepdims=True), 0.0), axis=1, keepdims=True)
        column = jnp.sum(jnp.where(r0 == r1, place_row(expert), 0.0), axis=1, keepdims=True)
        return weight * dot(jnp.where(column == spot, 1.0, 0.0).astype(BF16), contribution)

    mixed = hid[...]
    for j in (3, 2, 1):
        if j == 1:
            cut_stage(len(order) - 1)
            mixed = mixed + share_of(z, yzs[0])
        plane = partner(z, j)
        remote(yzs.at[j], yzr.at[j], yz_s.at[j], yz_r.at[j], unit(plane, c), x).wait_recv()
        mixed = mixed + share_of(plane, yzr[j])
    done = mixed.astype(BF16)
    fin[0] = done
    last = send(fin.at[0], fin.at[1], f_s, f_r, u, ox)
    out[:, half_of(x)] = done
    last.wait_recv()
    out[:, half_of(ox)] = fin[1]
    for copy in pending:
        copy.wait_send()


def layer(query, new_key, new_value, lengths, residual, gain, router_t, ids_t, key_cache, value_cache, out_w, gate_w, up_w, down_w):
    rows = residual.shape[0]
    block = residual.shape[1]
    half = block // CUTS
    cap = rows * 5 // 8
    hidden_units = gate_w.shape[1]
    count = PLANES * CORES * CUTS
    vmem = pl.BlockSpec(memory_space=pltpu.VMEM)
    hbm = pl.BlockSpec(memory_space=pl.ANY)
    dma = pltpu.SemaphoreType.DMA
    return pl.pallas_call(
        layer_kernel,
        out_shape=jax.ShapeDtypeStruct((rows, block), BF16),
        in_specs=[vmem] * 3 + [pl.BlockSpec(memory_space=pltpu.SMEM)] + [vmem] * 4 + [hbm] * 6,
        out_specs=vmem,
        scratch_shapes=[
            pltpu.VMEM(out_w.shape, BF16),
            pltpu.VMEM((W_SLOTS, block, hidden_units), BF16),
            pltpu.VMEM((W_SLOTS, block, hidden_units), BF16),
            pltpu.VMEM((D_SLOTS, hidden_units, block), BF16),
            pltpu.VMEM((query.shape[0], query.shape[1] // HD, HD), F32),
            pltpu.VMEM((2, query.shape[0], query.shape[1] // HD // 2, HD), F32),
            pltpu.VMEM(new_key.shape, F32),
            pltpu.VMEM(new_value.shape, F32),
            pltpu.VMEM((rows, query.shape[1]), BF16),
            pltpu.VMEM((rows, half), BF16),
            pltpu.VMEM((rows, half), BF16),
            pltpu.VMEM((rows, half), F32),
            pltpu.VMEM((PLANES, cap, half), BF16),
            pltpu.VMEM((cap, D), BF16),
            pltpu.VMEM((cap, hidden_units), F32),
            pltpu.VMEM((cap, hidden_units), F32),
            pltpu.VMEM((cap, hidden_units), BF16),
            pltpu.VMEM((PLANES, cap, block), BF16),
            pltpu.VMEM((PLANES, cap, block), BF16),
            pltpu.VMEM((PLANES, cap, half), BF16),
            pltpu.VMEM((PLANES, cap, half), BF16),
            pltpu.VMEM((PLANES, cap, half), BF16),
            pltpu.VMEM((PLANES, cap, half), BF16),
            pltpu.VMEM((2, rows, half), BF16),
            pltpu.VMEM((8, rows), F32),
            pltpu.VMEM((count, 8, rows), F32),
            dma(()), dma((W_SLOTS,)), dma((W_SLOTS,)), dma((D_SLOTS,)), dma((D_SLOTS, 8)),
            dma((8,)), dma((8,)), dma((8,)), dma((8,)), dma(()), dma(()),
            dma((4,)), dma((4,)), dma((4,)), dma((4,)), dma((8,)), dma((8,)),
            dma((count,)), dma((count,)),
            dma((4,)), dma((4,)), dma((4,)), dma((4,)), dma((4,)), dma((4,)),
            dma(()), dma(()),
        ],
        compiler_params=pltpu.CompilerParams(
            collective_id=0, has_side_effects=True, vmem_limit_bytes=VMEM_MIB * 2**20
        ),
        name="layer",
    )(query, new_key, new_value, lengths, residual, gain, router_t, ids_t, key_cache, value_cache, out_w, gate_w, up_w, down_w)


VMEM_MIB = 62


def fused_shards(
    residual, query, key_cache, value_cache, new_key, new_value, lengths, out_weight,
    router_weight, norm_gain, expert_ids, gate_weight, up_weight, down_weight,
):
    return layer(
        query, new_key, new_value, lengths, residual, norm_gain, router_weight.T, expert_ids.T,
        key_cache, value_cache, out_weight, gate_weight, up_weight, down_weight,
    )


def solution(mesh):
    placed = (
        P("groups", "units"),
        P(("groups", "units"), "cuts"),
        P(("groups", "units"), None, "cuts"),
        P(("groups", "units"), None, "cuts"),
        P(("groups", "units"), "cuts"),
        P(("groups", "units"), "cuts"),
        P(("groups", "units")),
        P("cuts", "units"),
        P("units", None),
        P("units"),
        P("groups", None),
        P(None, ("units", "cuts")),
        P(None, ("units", "cuts")),
        P(("units", "cuts"), None),
    )
    fits = (mesh.shape["units"], mesh.shape["cuts"]) == (PLANES * CORES, CUTS)
    return jax.shard_map(
        fused_shards if fits else shards, mesh=mesh, in_specs=placed, out_specs=P("groups", "units"), check_vma=False
    )
```
